256 devices in a mesh: seq: 16 (over z_hi, y, core), pipe: 16 (over x, z_lo).
Axes of the slice: x: 4, y: 4, z: 8 (z_hi: 2, z_lo: 4; z = z_hi * 4 + z_lo), core: 2. Of those that a mesh axis runs over, the one named last changes fastest.
Arguments:
- acts: bfloat16 [16, 2048, 2048], P('pipe', 'seq'), may hold values from -6 to 6
- norm_gain: float32 [16, 2048], P('pipe'), may hold values from 0.25 to 1.75
- query_weight: bfloat16 [16, 2048, 2048], P('pipe', None, 'seq'), may hold values from -64 to 64
- kv_weight: bfloat16 [16, 2048, 1024], P('pipe', None, 'seq'), may hold values from -64 to 64
- out_weight: bfloat16 [16, 2048, 2048], P('pipe', 'seq'), may hold values from -0.125 to 0.125
- first_values: bfloat16 [16, 2048, 512], P('pipe', 'seq'), may hold values from -6 to 6
- mix_weight: float32 [16, 8], P('pipe'), may hold values from 0.2 to 0.8
Outputs:
- passed: bfloat16 [16, 2048, 2048], P('pipe', 'seq')
- fresh_values: bfloat16 [16, 2048, 512], P('pipe', 'seq')
The draws below stay inside these ranges and needn't reach their ends.
All inputs are finite; a program needn't handle non-finite values.
Results may differ from the reference program's by a relative error of at most 0.011.
Values may be sent and summed in bfloat16 or wider, within the bound.
No kernel may reach another device: no remote copies, remote signals or barrier semaphores. Data moves between devices by JAX's collectives and lax.ppermute only.
A program may use at most 128 MiB of HBM per device.

```python
import math
import jax
import jax.numpy as jnp
from jax import lax

D = 2048
H = 32
HD = 64
KV = 8
QD = 2048
KVD = 512
TOKENS = 2048
N_PIPE = 16


def shared_basis(key):
    return jax.random.normal(key, (N_PIPE, D, H * HD), jnp.float32) / math.sqrt(D)


def draw_query_weight(key, part):
    basis = shared_basis(key)
    return basis.astype(jnp.bfloat16)


def draw_kv_weight(key, part):
    key = jax.random.fold_in(key, 23)
    key_noise, key_vals = jax.random.split(key, 2)
    noise = jax.random.normal(key_noise, (N_PIPE, D, KV * HD), jnp.float32) / math.sqrt(D)
    value_cols = jax.random.normal(key_vals, (N_PIPE, D, KV * HD), jnp.float32) / math.sqrt(D)
    key_cols = 2.5 * noise
    return jnp.concatenate([key_cols, value_cols], axis=-1).astype(jnp.bfloat16)


def block_scale(own_key, dims, cuts, least, high):
    loudness, own = 1.0, jax.random.fold_in(own_key, 6)
    for position, shards_of in cuts:
        heights = jnp.exp(jax.random.uniform(jax.random.fold_in(own, position), (shards_of,), jnp.float32, least / len(cuts), high / len(cuts)))
        loudness = loudness * jnp.repeat(heights, dims[position] // shards_of).reshape([-1 if axis == position else 1 for axis in range(len(dims))])
    return loudness


def centred(own_key, dims, scale, limit, cuts=(), kind=jnp.bfloat16):
    loudness = block_scale(own_key, dims, cuts, -0.22, 0.18) if cuts else 1.0
    array = jax.random.normal(own_key, dims, jnp.float32) * scale * loudness
    return jnp.minimum(jnp.maximum(array, -limit), limit).astype(kind)


def setup_inputs(seed: int = 0) -> dict:
    seeds = jax.random.split(jax.random.key(seed), 8)
    return {
        "acts": centred(seeds[0], (N_PIPE, TOKENS, D), 1.0, 6.0, ((0, 16), (1, 16))),
        "norm_gain": jnp.clip(1.0 + 0.15 * jax.random.normal(seeds[1], (N_PIPE, D), jnp.float32), 0.25, 1.75),
        "query_weight": draw_query_weight(jax.random.fold_in(seeds[7], 71), 0),
        "kv_weight": draw_kv_weight(jax.random.fold_in(seeds[7], 71), 0),
        "out_weight": centred(seeds[4], (N_PIPE, QD, D), QD ** -0.5, 0.125, ((0, 16), (1, 16))),
        "first_values": centred(seeds[5], (N_PIPE, TOKENS, KVD), 1.0, 6.0, ((0, 16), (1, 16))),
        "mix_weight": jnp.clip(0.2 + 0.6 * jax.random.uniform(seeds[6], (N_PIPE, KV), jnp.float32) ** block_scale(seeds[6], (N_PIPE, KV), ((0, 16),), -0.2, 0.2), 0.2, 0.8),
    }


rope_base = 500000.0

def block_rows(all_rows):
    if all_rows >= 4096:
        return all_rows // 8
    if all_rows % 512 == 0:
        return 512
    return all_rows

def normalize(inputs, gain):
    wide = inputs.astype(jnp.float32)
    scale = lax.rsqrt(lax.optimization_barrier(jnp.mean(wide * wide, axis=-1, keepdims=True)) + 1e-05)
    return (wide * scale * gain).astype(jnp.bfloat16)

def rotate(heads_in, positions):
    width = heads_in.shape[-1]
    half = width // 2
    freq = rope_base ** (-2.0 * jnp.arange(half, dtype=jnp.float32) / width)
    angle = positions.astype(jnp.float32)[:, None, None] * freq
    cosine = jnp.cos(angle)
    sine = jnp.sin(angle)
    lower = heads_in[..., :half]
    upper = heads_in[..., half:]
    return jnp.concatenate([lower * cosine - upper * sine, upper * cosine + lower * sine], axis=-1)

def head_attention(operands):
    query_head, key_head, value_head = operands
    all_rows = query_head.shape[0]
    block = block_rows(all_rows)
    scale = HD ** (-0.5)
    pieces = []
    for begin in range(0, all_rows, block):
        scores = jnp.dot(query_head[begin:begin + block], key_head.T, preferred_element_type=jnp.float32) * scale
        row_ids = begin + jnp.arange(block, dtype=jnp.int32)[:, None]
        col_ids = jnp.arange(all_rows, dtype=jnp.int32)[None, :]
        scores = jnp.where(col_ids <= row_ids, scores, -1e+30)
        top_score = lax.optimization_barrier(jnp.max(scores, axis=-1, keepdims=True))
        weights = jnp.exp(scores - top_score)
        probs = (weights / lax.optimization_barrier(jnp.sum(weights, axis=-1, keepdims=True))).astype(jnp.bfloat16)
        pieces.append(jnp.dot(probs, value_head, preferred_element_type=jnp.float32).astype(jnp.bfloat16))
    return jnp.concatenate(pieces, axis=0)

def section_layer(operands):
    inputs, gain, w_query, w_keyval, w_out, cached, mixing, is_first = operands
    all_rows = inputs.shape[0]
    normed = normalize(inputs, gain)
    positions = jnp.arange(all_rows, dtype=jnp.int32)
    queries = rotate(jnp.dot(normed, w_query, preferred_element_type=jnp.float32).reshape(all_rows, H, HD), positions).astype(jnp.bfloat16)
    keyval = jnp.dot(normed, w_keyval, preferred_element_type=jnp.float32)
    keys_rot = rotate(keyval[:, :KVD].reshape(all_rows, KV, HD), positions).astype(jnp.bfloat16)
    values = keyval[:, KVD:].astype(jnp.bfloat16)
    first_vals = jnp.where(is_first, values, cached)
    lam_cols = jnp.repeat(mixing, HD)
    mixed_vals = (lam_cols * values.astype(jnp.float32) + (1.0 - lam_cols) * first_vals.astype(jnp.float32)).astype(jnp.bfloat16)
    mixed_vals = mixed_vals.reshape(all_rows, KV, HD)
    group = H // KV
    query_major = jnp.transpose(queries, (1, 0, 2))
    key_major = jnp.transpose(jnp.repeat(keys_rot, group, axis=1), (1, 0, 2))
    value_major = jnp.transpose(jnp.repeat(mixed_vals, group, axis=1), (1, 0, 2))
    attended = lax.map(head_attention, (query_major, key_major, value_major))
    attended = jnp.transpose(attended, (1, 0, 2)).reshape(all_rows, H * HD)
    layer_out = inputs.astype(jnp.float32) + jnp.dot(attended, w_out, preferred_element_type=jnp.float32)
    return (layer_out.astype(jnp.bfloat16), values)

def reference(acts, norm_gain, query_weight, kv_weight, out_weight, first_values, mix_weight):
    is_first = jnp.arange(N_PIPE, dtype=jnp.int32) == 0
    layer_outs, section_values = lax.map(section_layer, (acts, norm_gain, query_weight, kv_weight, out_weight, first_values, mix_weight, is_first))
    passed = jnp.roll(layer_outs, 1, axis=0)
    fresh_values = jnp.broadcast_to(section_values[0], section_values.shape)
    return (passed, fresh_values)
```

```python
import functools

import jax
import jax.numpy as jnp
from jax import lax
from jax.experimental import pallas as pl
from jax.experimental.pallas import tpu as pltpu
from jax.sharding import Mesh
from jax.sharding import PartitionSpec as P

HALVES, RING, CORES, XS, ZS = 2, 4, 2, 4, 4
SEQ = ("zh", "y", "c")
PIPE = ("x", "zl")
rope_base = 500000.0
F32 = jnp.float32
BF16 = jnp.bfloat16
CHUNK = 256


def normalize(inputs, gain):
    wide = inputs.astype(F32)
    scale = lax.rsqrt(jnp.mean(wide * wide, axis=-1, keepdims=True) + 1e-05)
    return (wide * scale * gain).astype(BF16)


def pull(x, axis, by):
    n = lax.axis_size(axis)
    return lax.ppermute(x, axis, [((i + by) % n, i) for i in range(n)])


def rope_tables(positions, head_dim):
    half = head_dim // 2
    freq = rope_base ** (-2.0 * jnp.arange(half, dtype=F32) / head_dim)
    angle = positions.astype(F32)[:, None] * freq
    cosine, sine = jnp.cos(angle), jnp.sin(angle)
    return (
        jnp.concatenate([cosine] * 4, axis=-1),
        jnp.concatenate([-sine, sine, -sine, sine], axis=-1),
    )


def rope(u, cosine, sine):
    lanes = lax.broadcasted_iota(jnp.int32, u.shape, 1)
    swapped = jnp.where(lanes % 64 < 32, pltpu.roll(u, 96, 1), pltpu.roll(u, 32, 1))
    return u * cosine + swapped * sine


def keyval_kernel(place, x, wa, wb, pa, pb, cos, sin, first, mix, kv_out, val_out, w):
    y, h, c, section = place[0], place[1], place[2], place[3]
    w[0:64], w[64:128], w[128:192], w[192:256] = wa[...], pa[...], wb[...], pb[...]
    both = lax.dot_general(x[...], w[...], (((1,), (1,)), ((), ())), preferred_element_type=F32)
    rows = 128
    for slot in range(RING):
        part = both[slot * rows : (slot + 1) * rows]
        own, other = part[:, :128], part[:, 128:]
        keys = jnp.where(h == 0, own, other)
        values = jnp.where(h == 0, other, own)
        keys = jnp.where(c == 0, keys, pltpu.roll(keys, 64, 1))
        values = jnp.where(c == 0, values, pltpu.roll(values, 64, 1))
        rounded = values.astype(BF16)
        wide = rounded.astype(F32)
        before = jnp.where(section == 0, wide, first[slot].astype(F32))
        mixed = mix[0:1, :] * wide + (1.0 - mix[0:1, :]) * before
        keys = rope(keys, cos[slot], sin[slot])
        lanes = lax.broadcasted_iota(jnp.int32, keys.shape, 1)
        low = jnp.where(lanes < 64, keys, pltpu.roll(mixed, 64, 1))
        high = jnp.where(lanes < 64, pltpu.roll(keys, 64, 1), mixed)
        at = lax.rem(y + slot, RING)
        kv_out[at, :, 0:128] = low.astype(BF16)
        kv_out[at, :, 128:256] = high.astype(BF16)
        val_out[slot] = rounded


def query_kernel(x, wa, wb, cos, sin, out, w):
    w[:, :128], w[:, 128:] = wa[...], wb[...]
    both = jnp.dot(x[...], w[...], preferred_element_type=F32)
    for slot in range(RING):
        part = both[slot * 128 : (slot + 1) * 128]
        for pair in range(2):
            u = rope(part[:, pair * 128 : (pair + 1) * 128], cos[slot], sin[slot])
            out[slot, :, pair * 128 : (pair + 1) * 128] = (u * 0.125).astype(BF16)


def attend_kernel(place, q, kv, out, keys, vals, scores, q4):
    step = pl.program_id(0)
    h, c = place[1], place[2]
    lanes = lax.broadcasted_iota(jnp.int32, (128, 128), 1)

    @pl.when(step == 0)
    def _():
        both = kv[...].astype(F32)
        turned = pltpu.roll(both, 64, 1)
        lane = lax.broadcasted_iota(jnp.int32, both.shape, 1)
        keys[...] = jnp.where(lane < 64, both, turned).astype(BF16)
        vals[...] = jnp.where(lane < 64, turned, 1.0).astype(BF16)

    for pair in range(2):
        block = q[0, :, pair * 128 : (pair + 1) * 128].astype(F32)
        q4[pair * 256 : pair * 256 + 128] = jnp.where(lanes < 64, block, 0.0).astype(BF16)
        q4[pair * 256 + 128 : pair * 256 + 256] = jnp.where(lanes < 64, 0.0, block).astype(BF16)
    count = h * 4 + step + 1

    def dots(j):
        chunk = keys[pl.ds(pl.multiple_of(j * CHUNK, CHUNK), CHUNK), :]
        return lax.dot_general(q4[...], chunk, (((1,), (1,)), ((), ())), preferred_element_type=F32)

    s = dots(count - 1)
    row = lax.rem(lax.broadcasted_iota(jnp.int32, s.shape, 0), 128) + c * 128
    col = lax.broadcasted_iota(jnp.int32, s.shape, 1)
    s = jnp.where(col <= row, s, -1e30)
    scores[count - 1] = s
    top = jnp.maximum(s[:, :128], s[:, 128:])

    def first_pass(j, top):
        s = dots(j)
        scores[j] = s
        return jnp.maximum(top, jnp.maximum(s[:, :128], s[:, 128:]))

    top = lax.fori_loop(0, count - 1, first_pass, top)
    top = jnp.max(top, axis=1, keepdims=True)

    def second_pass(j, acc):
        p = jnp.exp(scores[j] - top).astype(BF16)
        chunk = vals[pl.ds(pl.multiple_of(j * CHUNK, CHUNK), CHUNK), :]
        return acc + jnp.dot(p, chunk, preferred_element_type=F32)

    acc = lax.fori_loop(0, count, second_pass, jnp.zeros((512, 128), F32))
    result = acc / pltpu.roll(acc, 64, 1)
    for pair in range(2):
        left = result[pair * 256 : pair * 256 + 128]
        right = pltpu.roll(result[pair * 256 + 128 : pair * 256 + 256], 64, 1)
        out[0, :, pair * 128 : (pair + 1) * 128] = jnp.where(lanes < 64, left, right).astype(BF16)


def out_kernel(base, *refs):
    att, weights, out = refs[:4], refs[4:12], refs[12]
    total = base[...].astype(F32)
    for k in range(4):
        for pair in range(2):
            total += jnp.dot(
                att[k][:, pair * 128 : (pair + 1) * 128], weights[2 * k + pair][...], preferred_element_type=F32
            )
    out[...] = total.astype(out.dtype)


def params(mib):
    return pltpu.CompilerParams(vmem_limit_bytes=mib * 2**20)


VM = pl.BlockSpec(memory_space=pltpu.VMEM)
SM = pl.BlockSpec(memory_space=pltpu.SMEM)


def keyval(place, x, wa, wb, pa, pb, cos, sin, first, mix):
    return pl.pallas_call(
        keyval_kernel,
        out_shape=(jax.ShapeDtypeStruct((4, 128, 256), BF16), jax.ShapeDtypeStruct((4, 128, 128), BF16)),
        in_specs=[SM] + [VM] * 9,
        out_specs=(VM, VM),
        scratch_shapes=[pltpu.VMEM((256, 2048), BF16)],
        compiler_params=params(24),
        cost_estimate=pl.CostEstimate(flops=2 * 512 * 2048 * 256, bytes_accessed=4 << 20, transcendentals=0),
    )(place, x, wa, wb, pa, pb, cos, sin, first, mix)


def query(x, wa, wb, cos, sin):
    return pl.pallas_call(
        query_kernel,
        out_shape=jax.ShapeDtypeStruct((4, 128, 256), BF16),
        in_specs=[VM] * 5,
        out_specs=VM,
        scratch_shapes=[pltpu.VMEM((2048, 256), BF16)],
        compiler_params=params(24),
        cost_estimate=pl.CostEstimate(flops=2 * 512 * 2048 * 256, bytes_accessed=4 << 20, transcendentals=0),
    )(x, wa, wb, cos, sin)


def attend(place, q, kv):
    def at(step, place):
        return (lax.rem(step - place[0] + RING, RING), 0, 0)

    return pl.pallas_call(
        attend_kernel,
        out_shape=jax.ShapeDtypeStruct((4, 128, 256), BF16),
        grid_spec=pltpu.PrefetchScalarGridSpec(
            num_scalar_prefetch=1,
            grid=(RING,),
            in_specs=[
                pl.BlockSpec((1, 128, 256), at),
                pl.BlockSpec((2048, 128), lambda step, place: (0, 0)),
            ],
            out_specs=pl.BlockSpec((1, 128, 256), at),
            scratch_shapes=[
                pltpu.VMEM((2048, 128), BF16),
                pltpu.VMEM((2048, 128), BF16),
                pltpu.VMEM((8, 512, CHUNK), F32),
                pltpu.VMEM((512, 128), BF16),
            ],
        ),
        compiler_params=params(24),
        cost_estimate=pl.CostEstimate(flops=2 * 2 * 512 * 128 * 6656, bytes_accessed=2 << 20, transcendentals=512 * 6656),
    )(place, q, kv)


def project_out(base, att, weights, dtype):
    return pl.pallas_call(
        out_kernel,
        out_shape=jax.ShapeDtypeStruct(base.shape, dtype),
        in_specs=[VM] * 13,
        out_specs=VM,
        compiler_params=params(24),
        cost_estimate=pl.CostEstimate(flops=2 * 128 * 1024 * 2048, bytes_accessed=6 << 20, transcendentals=0),
    )(base, *att, *weights)


def per_device(acts, norm_gain, query_weight, kv_weight, out_weight, first_values, mix_weight):
    inputs = acts[0]
    tok = inputs.shape[0]
    h, y, c = lax.axis_index("zh"), lax.axis_index("y"), lax.axis_index("c")
    section = lax.axis_index("x") * ZS + lax.axis_index("zl")
    place = jnp.stack([y, h, c, section]).astype(jnp.int32)
    core = functools.partial(pull, axis="c", by=1)
    half = functools.partial(pull, axis="zh", by=1)

    w_kv = kv_weight[0].T
    home = [(s, s // 8 * 8 + s % 4 * 2 + s % 8 // 4) for s in range(16)]
    kv_a = lax.ppermute(w_kv, SEQ, home)
    kv_b = lax.ppermute(w_kv, SEQ, [(s, (d + 8) % 16) for s, d in home])
    kv_pa, kv_pb = core(kv_a), core(kv_b)

    normed = normalize(inputs, norm_gain[0])
    x = jnp.concatenate([normed] + [pull(normed, "y", k) for k in range(1, RING)], axis=0)

    w_q = query_weight[0]
    q_c = core(w_q)
    q_z = half(w_q)
    q_zc = core(q_z)

    slots = [lax.rem(y + k, RING) for k in range(RING)]
    positions = jnp.concatenate([(h * 8 + s * 2 + c) * tok + jnp.arange(tok, dtype=jnp.int32) for s in slots])
    cos, sin = (t.reshape(RING, tok, 128) for t in rope_tables(positions, 64))

    cached = jnp.transpose(first_values[0].reshape(tok, 2, RING, 64), (2, 0, 1, 3)).reshape(RING, tok, 128)
    pieces = [lax.dynamic_index_in_dim(cached, y, 0, keepdims=False)]
    for k in range(1, RING):
        pieces.append(pull(lax.dynamic_index_in_dim(cached, lax.rem(y + RING - k, RING), 0, keepdims=False), "y", k))
    first = jnp.stack(pieces)
    mix_two = lax.dynamic_index_in_dim(mix_weight[0].reshape(2, RING), y, 1, keepdims=False)
    mix = jnp.broadcast_to(jnp.repeat(mix_two, 64)[None, :], (8, 128))

    kv, values = keyval(place, x, kv_a, kv_b, kv_pa, kv_pb, cos, sin, first, mix)

    def paired(mine, theirs):
        pair = jnp.where(c == 0, jnp.stack([mine, theirs], 1), jnp.stack([theirs, mine], 1))
        return pair.reshape(RING * 2 * tok, 256)

    kv_before = lax.ppermute(kv, "zh", [(0, 1)])
    own = paired(kv, core(kv))
    before = paired(kv_before, core(kv_before))
    kv_all = jnp.concatenate([jnp.where(h == 0, own, before), own], axis=0)
    kv_low, kv_high = kv_all[:, :128], kv_all[:, 128:]
    kv_near = jnp.where(h == 0, kv_low, kv_high)
    kv_far = jnp.where(h == 0, kv_high, kv_low)

    q_near = query(x, w_q, q_c, cos, sin)
    att_near = attend(place, q_near, kv_near)
    near = [att_near[0]] + [pull(att_near[k], "y", RING - k) for k in range(1, RING)]

    q_far = query(x, q_z, q_zc, cos, sin)
    att_far = attend(place, q_far, kv_far)
    far = [att_far[0]] + [pull(att_far[k], "y", RING - k) for k in range(1, RING)]

    def rows_of(w):
        blocks = [w] + [pull(w, "y", RING - k) for k in range(1, RING)]
        return [b for block in blocks for b in (block, core(block))]

    w_o = out_weight[0]
    total = project_out(inputs, near, rows_of(w_o), F32)
    layer_out = project_out(total, far, rows_of(half(w_o)), BF16)
    passed = pull(layer_out, PIPE, XS * ZS - 1)

    back = [values[0]] + [pull(values[k], "y", RING - k) for k in range(1, RING)]
    turned = jnp.stack(back[::-1])
    turned = jnp.roll(turned, y + 1, axis=0).reshape(RING, tok, 2, 64)
    fresh = jnp.transpose(turned, (1, 2, 0, 3)).reshape(tok, 512)
    fresh = jnp.where(section == 0, fresh, jnp.zeros_like(fresh))
    for pairs in (
        [(0, 2)],
        [(0, 1), (2, 3)],
        [(p, p + 4) for p in range(4)],
        [(p, p + 12) for p in range(4)] + [(p + 4, p + 8) for p in range(4)],
    ):
        fresh = fresh + lax.ppermute(fresh, PIPE, pairs)
    return (passed[None], fresh[None])


def solution(mesh):
    split = Mesh(mesh.devices.reshape(HALVES, RING, CORES, XS, ZS), SEQ + PIPE)
    placed = (
        P(PIPE, SEQ, None),
        P(PIPE, None),
        P(PIPE, None, SEQ),
        P(PIPE, None, SEQ),
        P(PIPE, SEQ, None),
        P(PIPE, SEQ, None),
        P(PIPE, None),
    )
    return jax.shard_map(
        per_device,
        mesh=split,
        in_specs=placed,
        out_specs=(P(PIPE, SEQ, None), P(PIPE, SEQ, None)),
        check_vma=False,
    )
```

```python
import functools

import jax
import jax.numpy as jnp
from jax import lax
from jax.experimental import pallas as pl
from jax.experimental.pallas import tpu as pltpu
from jax.sharding import Mesh
from jax.sharding import PartitionSpec as P

HALVES, RING, CORES, XS, ZS = 2, 4, 2, 4, 4
SEQ = ("zh", "y", "c")
PIPE = ("x", "zl")
rope_base = 500000.0
F32 = jnp.float32
BF16 = jnp.bfloat16
CHUNK = 512


def prepare_kernel(acts, gain, first, out):
    wide = acts[...].astype(F32)
    scale = lax.rsqrt(jnp.mean(wide * wide, axis=-1, keepdims=True) + 1e-05)
    normed = (wide * scale * gain[...]).astype(BF16)
    lanes = lax.broadcasted_iota(jnp.int32, (acts.shape[0], 128), 1)
    for to in range(RING):
        out[to, :, :2048] = normed
        at = to // 2 * 128
        low = first[:, at : at + 128].astype(F32)
        high = first[:, 256 + at : 384 + at].astype(F32)
        if to % 2 == 0:
            high = pltpu.roll(high, 64, 1)
        else:
            low = pltpu.roll(low, 64, 1)
        out[to, :, 2048:] = jnp.where(lanes < 64, low, high).astype(BF16)


def pull(x, axis, by):
    n = lax.axis_size(axis)
    return lax.ppermute(x, axis, [((i + by) % n, i) for i in range(n)])


def rope_tables(positions, head_dim):
    half = head_dim // 2
    freq = rope_base ** (-2.0 * jnp.arange(half, dtype=F32) / head_dim)
    angle = positions.astype(F32)[:, None] * freq
    cosine, sine = jnp.cos(angle), jnp.sin(angle)
    return (
        jnp.concatenate([cosine] * 4, axis=-1),
        jnp.concatenate([-sine, sine, -sine, sine], axis=-1),
    )


def rope(u, cosine, sine):
    lanes = lax.broadcasted_iota(jnp.int32, u.shape, 1)
    swapped = jnp.where(lanes % 64 < 32, pltpu.roll(u, 96, 1), pltpu.roll(u, 32, 1))
    return u * cosine + swapped * sine


def keyval_kernel(place, x, mine, theirs, cos, sin, mix, *refs):
    kv_out, val_out, w = refs[-3:]
    h, c, section = place[1], place[2], place[3]
    w[0:64], w[64:128], w[128:192], w[192:256] = mine[0:64], theirs[0:64], mine[64:128], theirs[64:128]
    both = lax.dot_general(x[:, :2048], w[...], (((1,), (1,)), ((), ())), preferred_element_type=F32)
    rows = 128
    for slot in range(RING):
        part = both[slot * rows : (slot + 1) * rows]
        own, other = part[:, :128], part[:, 128:]
        keys = jnp.where(h == 0, own, other)
        values = jnp.where(h == 0, other, own)
        keys = jnp.where(c == 0, keys, pltpu.roll(keys, 64, 1))
        values = jnp.where(c == 0, values, pltpu.roll(values, 64, 1))
        rounded = values.astype(BF16)
        wide = rounded.astype(F32)
        before = jnp.where(section == 0, wide, x[slot * rows : (slot + 1) * rows, 2048:].astype(F32))
        mixed = mix[0:1, :] * wide + (1.0 - mix[0:1, :]) * before
        keys = rope(keys, cos[slot], sin[slot])
        lanes = lax.broadcasted_iota(jnp.int32, keys.shape, 1)
        low = jnp.where(lanes < 64, keys, pltpu.roll(mixed, 64, 1))
        high = jnp.where(lanes < 64, pltpu.roll(keys, 64, 1), mixed)
        kv_out[slot, :, 0:128] = low.astype(BF16)
        kv_out[slot, :, 128:256] = high.astype(BF16)
        val_out[slot] = rounded


def query_kernel(x, wa, wb, cos, sin, out, w):
    w[:, :128], w[:, 128:] = wa[...], wb[...]
    both = jnp.dot(x[:, :2048], w[...], preferred_element_type=F32)
    for slot in range(RING):
        part = both[slot * 128 : (slot + 1) * 128]
        for pair in range(2):
            u = rope(part[:, pair * 128 : (pair + 1) * 128], cos[slot], sin[slot])
            out[slot, :, pair * 128 : (pair + 1) * 128] = (u * 0.125).astype(BF16)


def attend_kernel(place, q, kv, kv_c, before, before_c, *refs):
    out, keys, vals, scores, q4 = refs[-5:]
    step = pl.program_id(0)
    h, c, head = place[1], place[2], pl.multiple_of(place[4], 128)
    lanes = lax.broadcasted_iota(jnp.int32, (128, 128), 1)

    def place_block(src, k, half, core):
        both = src[k, :, pl.ds(head, 128)].astype(F32)
        turned = pltpu.roll(both, 64, 1)
        at = pl.ds(pl.multiple_of(half * 1024 + k * 256 + core * 128, 128), 128)
        keys[:, at] = jnp.where(lanes < 64, both, turned).T.astype(BF16)
        vals[at, :] = jnp.where(lanes < 64, turned, 1.0).astype(BF16)

    @pl.when(step == 0)
    def _():
        for k in range(RING):
            place_block(kv, k, h, c)
            place_block(kv_c, k, h, 1 - c)

    @pl.when((step == 0) & (h == 1))
    def _():
        for k in range(RING):
            place_block(before, k, 0, c)
            place_block(before_c, k, 0, 1 - c)

    for pair in range(2):
        block = q[0, :, pair * 128 : (pair + 1) * 128].astype(F32)
        q4[pair * 256 : pair * 256 + 128] = jnp.where(lanes < 64, block, 0.0).astype(BF16)
        q4[pair * 256 + 128 : pair * 256 + 256] = jnp.where(lanes < 64, 0.0, block).astype(BF16)
    last = h * (1024 // CHUNK) + step * 256 // CHUNK

    def dots(j):
        chunk = keys[:, pl.ds(pl.multiple_of(j * CHUNK, CHUNK), CHUNK)]
        return jnp.dot(q4[...], chunk, preferred_element_type=F32)

    def greatest(s):
        top = s[:, :128]
        for k in range(1, CHUNK // 128):
            top = jnp.maximum(top, s[:, k * 128 : (k + 1) * 128])
        return top

    s = dots(last)
    row = lax.rem(lax.broadcasted_iota(jnp.int32, s.shape, 0), 128) + c * 128 + lax.rem(step * 256, CHUNK)
    col = lax.broadcasted_iota(jnp.int32, s.shape, 1)
    s = jnp.where(col <= row, s, -1e30)
    scores[last] = s

    def first_pass(j, top):
        s = dots(j)
        scores[j] = s
        return jnp.maximum(top, greatest(s))

    top = lax.fori_loop(0, last, first_pass, greatest(s))
    top = jnp.max(top, axis=1, keepdims=True)

    def second_pass(j, acc):
        p = jnp.exp(scores[j] - top).astype(BF16)
        chunk = vals[pl.ds(pl.multiple_of(j * CHUNK, CHUNK), CHUNK), :]
        return acc + jnp.dot(p, chunk, preferred_element_type=F32)

    acc = lax.fori_loop(0, last + 1, second_pass, jnp.zeros((512, 128), F32))
    result = acc / pltpu.roll(acc, 64, 1)
    for pair in range(2):
        left = result[pair * 256 : pair * 256 + 128]
        right = pltpu.roll(result[pair * 256 + 128 : pair * 256 + 256], 64, 1)
        out[0, :, pair * 128 : (pair + 1) * 128] = jnp.where(lanes < 64, left, right).astype(BF16)


def gather_heads_kernel(place, parts, out):
    lanes = lax.broadcasted_iota(jnp.int32, (128, 128), 1)
    keep = jnp.where(place[3] == 0, 1.0, 0.0)
    for k in range(0, RING, 2):
        left, right = parts[k].astype(F32) * keep, parts[k + 1].astype(F32) * keep
        at = k // 2 * 128
        out[:, at : at + 128] = jnp.where(lanes < 64, left, pltpu.roll(right, 64, 1)).astype(BF16)
        out[:, 256 + at : 384 + at] = jnp.where(lanes < 64, pltpu.roll(left, 64, 1), right).astype(BF16)


def partial_sums(att, beside, weights):
    total = 0.0
    for k, w in enumerate(weights):
        blocks = (att[0:2] if k < 2 else beside[...]).reshape(256, 256)
        total += jnp.dot(blocks[:, k % 2 * 128 : k % 2 * 128 + 128], w[...], preferred_element_type=F32)
    return total


def out_near_kernel(att, beside, w0, w1, w2, w3, *refs):
    refs[-1][...] = partial_sums(att, beside, (w0, w1, w2, w3))


def out_far_kernel(place, acts, base, att, beside, w0, w1, w2, w3, mine, theirs):
    odd = lax.rem(place[0], 2)
    total = base[...] + partial_sums(att, beside, (w0, w1, w2, w3))
    low, high = total[:128], total[128:]
    mine[...] = (acts[...].astype(F32) + jnp.where(odd == 0, low, high)).astype(BF16)
    theirs[...] = jnp.where(odd == 0, high, low).astype(BF16)


def params(mib):
    return pltpu.CompilerParams(vmem_limit_bytes=mib * 2**20)


VM = pl.BlockSpec(memory_space=pltpu.VMEM)
SM = pl.BlockSpec(memory_space=pltpu.SMEM)


def prepare(acts, gain, first):
    return pl.pallas_call(
        prepare_kernel,
        out_shape=jax.ShapeDtypeStruct((RING, acts.shape[0], 2048 + 128), BF16),
        in_specs=[VM] * 3,
        out_specs=VM,
        compiler_params=params(16),
        cost_estimate=pl.CostEstimate(flops=2 * 512 * 2048 * 256, bytes_accessed=4 << 20, transcendentals=0),
    )(acts, gain, first)


def keyval(operands, *others):
    return pl.pallas_call(
        keyval_kernel,
        out_shape=(jax.ShapeDtypeStruct((4, 128, 256), BF16), jax.ShapeDtypeStruct((4, 128, 128), BF16)),
        in_specs=[SM] + [VM] * 6 + [pl.BlockSpec(memory_space=pl.ANY)] * len(others),
        out_specs=(VM, VM),
        scratch_shapes=[pltpu.VMEM((256, 2048), BF16)],
        compiler_params=params(24),
        cost_estimate=pl.CostEstimate(flops=2 * 512 * 2048 * 256, bytes_accessed=4 << 20, transcendentals=0),
    )(*operands, *others)


def query(x, wa, wb, cos, sin):
    return pl.pallas_call(
        query_kernel,
        out_shape=jax.ShapeDtypeStruct((4, 128, 256), BF16),
        in_specs=[VM] * 5,
        out_specs=VM,
        scratch_shapes=[pltpu.VMEM((2048, 256), BF16)],
        compiler_params=params(24),
        cost_estimate=pl.CostEstimate(flops=2 * 512 * 2048 * 256, bytes_accessed=4 << 20, transcendentals=0),
    )(x, wa, wb, cos, sin)


def attend(place, q, kvs, *others):
    def at(step, place):
        return (step, 0, 0)

    def to(step, place):
        return (lax.rem(step + place[0] // 2 * 2, RING), 0, 0)

    return pl.pallas_call(
        attend_kernel,
        out_shape=jax.ShapeDtypeStruct((4, 128, 256), BF16),
        grid_spec=pltpu.PrefetchScalarGridSpec(
            num_scalar_prefetch=1,
            grid=(RING,),
            in_specs=[
                pl.BlockSpec((1, 128, 256), at),
            ]
            + [pl.BlockSpec((RING, 128, 256), lambda step, place: (0, 0, 0))] * 4
            + [pl.BlockSpec(memory_space=pl.ANY)] * len(others),
            out_specs=pl.BlockSpec((1, 128, 256), to),
            scratch_shapes=[
                pltpu.VMEM((128, 2048), BF16),
                pltpu.VMEM((2048, 128), BF16),
                pltpu.VMEM((2048 // CHUNK, 512, CHUNK), F32),
                pltpu.VMEM((512, 128), BF16),
            ],
        ),
        compiler_params=params(24),
        cost_estimate=pl.CostEstimate(flops=2 * 2 * 512 * 256 * 6656, bytes_accessed=32 << 20, transcendentals=512 * 6656),
    )(place, q, *kvs, *others)


def out_near(att, beside, weights, *others):
    return pl.pallas_call(
        out_near_kernel,
        out_shape=jax.ShapeDtypeStruct((256, 2048), F32),
        in_specs=[VM] * 6 + [pl.BlockSpec(memory_space=pl.ANY)] * len(others),
        out_specs=VM,
        compiler_params=params(24),
        cost_estimate=pl.CostEstimate(flops=2 * 512 * 2048 * 256, bytes_accessed=4 << 20, transcendentals=0),
    )(att, beside, *weights, *others)


def out_far(place, acts, base, att, beside, weights):
    return pl.pallas_call(
        out_far_kernel,
        out_shape=(jax.ShapeDtypeStruct(acts.shape, BF16),) * 2,
        in_specs=[SM] + [VM] * 8,
        out_specs=(VM, VM),
        compiler_params=params(24),
        cost_estimate=pl.CostEstimate(flops=2 * 512 * 2048 * 256, bytes_accessed=4 << 20, transcendentals=0),
    )(place, acts, base, att, beside, *weights)


def hold(arrays, *others):
    n = len(arrays)
    return pl.pallas_call(
        lambda *refs: None,
        out_shape=[jax.ShapeDtypeStruct(x.shape, x.dtype) for x in arrays],
        in_specs=[pl.BlockSpec(memory_space=pl.ANY)] * (n + len(others)),
        out_specs=[pl.BlockSpec(memory_space=pl.ANY)] * n,
        input_output_aliases={k: k for k in range(n)},
    )(*arrays, *others)


def gather_heads(place, parts):
    return pl.pallas_call(
        gather_heads_kernel,
        out_shape=jax.ShapeDtypeStruct((128, 512), BF16),
        in_specs=[SM, VM],
        out_specs=VM,
        cost_estimate=pl.CostEstimate(flops=0, bytes_accessed=1 << 18, transcendentals=0),
    )(place, parts)


def beside_b(x):
    return lax.ppermute(x, "y", [(y, RING - 1 - y) for y in range(RING)])


def swap(x):
    return lax.all_to_all(x, "y", 0, 0)


def per_device(acts, norm_gain, query_weight, kv_weight, out_weight, first_values, mix_weight):
    inputs = acts[0]
    tok = inputs.shape[0]
    h, y, c = lax.axis_index("zh"), lax.axis_index("y"), lax.axis_index("c")
    section = lax.axis_index("x") * ZS + lax.axis_index("zl")
    place = jnp.stack([y, h, c, section, 128 * h]).astype(jnp.int32)
    place_far = jnp.stack([y, h, c, section, 128 - 128 * h]).astype(jnp.int32)
    core = functools.partial(pull, axis="c", by=1)
    half = functools.partial(pull, axis="zh", by=1)

    positions = h * 8 * tok + (2 * jnp.arange(RING, dtype=jnp.int32)[:, None] + c) * tok + jnp.arange(tok, dtype=jnp.int32)
    cos, sin = (t.reshape(RING, tok, 128) for t in rope_tables(positions.reshape(-1), 64))
    mix_two = lax.dynamic_index_in_dim(mix_weight[0].reshape(2, RING), y, 1, keepdims=False)
    mix = jnp.broadcast_to(jnp.repeat(mix_two, 64)[None, :], (8, 128))

    x = swap(prepare(inputs, norm_gain, first_values[0]))

    w_kv = kv_weight[0].T
    home = [(s, s // 8 * 8 + s % 4 * 2 + s % 8 // 4) for s in range(16)]
    kv_b = lax.ppermute(w_kv, SEQ, [(s, (d + 8) % 16) for s, d in home])
    kv_a = lax.ppermute(w_kv, SEQ, home)
    mine = jnp.concatenate([kv_a, kv_b], axis=0)
    theirs = core(mine)

    w_q, w_o = query_weight[0], out_weight[0]
    q_z, q_c, o_c = half(w_q), core(w_q), core(w_o)
    x = x.reshape(RING * tok, 2048 + 128)
    kv, values = keyval((place, x, mine, theirs, cos, sin, mix), q_z, q_c, o_c)

    o_1, o_own = hold([w_o[: tok // 2], w_o], kv)
    kv_c = core(kv)
    kv_before = lax.ppermute(kv, "zh", [(0, 1)])
    kv_before_c = core(kv_before)
    kvs = (kv, kv_c, kv_before, kv_before_c)
    o_z1 = half(o_1)
    o_b = beside_b(o_own)
    fresh = gather_heads(place, swap(values))
    q_near = query(x, w_q, q_c, cos, sin)

    def sent_on(x, stride):
        return [lax.ppermute(x, PIPE, [(p, p + k * stride) for p in range(stride)]) for k in range(1, 4)]

    o_2, o_z1, o_b, q_z, fresh = hold([w_o[tok // 2 :], o_z1, o_b, q_z, fresh], kv_before_c)
    att_near = attend(place, q_near, kvs, o_b)
    o_z2 = half(o_2)
    o_zb1 = beside_b(o_z1)
    o_bc = core(o_b)
    q_zc = core(q_z)
    q_far = query(x, q_z, q_zc, cos, sin)

    o_z2, o_zb1, o_bc, q_far, fresh = hold([o_z2, o_zb1, o_bc, q_far, fresh], att_near)
    near = beside_b(att_near[2:4])
    o_zb2 = beside_b(o_z2)
    fresh = sum(sent_on(fresh, 1), fresh)
    att_far = attend(place_far, q_far, kvs)
    total = out_near(att_near, near, [w_o, o_c, o_b, o_bc], fresh)

    far = beside_b(att_far[2:4])
    (o_zb2,) = hold([o_zb2], att_far)
    rows = jnp.concatenate([o_z1, o_z2, o_zb1, o_zb2], axis=0)
    rows_c = core(rows)
    mine, theirs = out_far(place, inputs, total, att_far, far, [rows[:tok], rows_c[:tok], rows[tok:], rows_c[tok:]])
    (fresh,) = hold([fresh], mine)
    fresh = sum(sent_on(fresh, ZS), fresh)

    onward = [(p, (p + 1) % (XS * ZS)) for p in range(XS * ZS)]
    across = [(y * XS * ZS + p, (y ^ 1) * XS * ZS + q) for p, q in onward for y in range(RING)]
    sums = [lax.ppermute(theirs, ("y",) + PIPE, across), lax.ppermute(mine, PIPE, onward)]
    passed = (sums[0].astype(F32) + sums[1].astype(F32)).astype(BF16)
    return (passed[None], fresh[None])


def solution(mesh):
    split = Mesh(mesh.devices.reshape(HALVES, RING, CORES, XS, ZS), SEQ + PIPE)
    placed = (
        P(PIPE, SEQ, None),
        P(PIPE, None),
        P(PIPE, None, SEQ),
        P(PIPE, None, SEQ),
        P(PIPE, SEQ, None),
        P(PIPE, SEQ, None),
        P(PIPE, None),
    )
    return jax.shard_map(
        per_device,
        mesh=split,
        in_specs=placed,
        out_specs=(P(PIPE, SEQ, None), P(PIPE, SEQ, None)),
        check_vma=False,
    )
```

```python
import functools

import jax
import jax.numpy as jnp
from jax import lax
from jax.experimental import pallas as pl
from jax.experimental.pallas import tpu as pltpu
from jax.sharding import Mesh
from jax.sharding import PartitionSpec as P

HALVES, RING, CORES, XS, ZS = 2, 4, 2, 4, 4
SEQ = ("zh", "y", "c")
PIPE = ("x", "zl")
rope_base = 500000.0
F32 = jnp.float32
BF16 = jnp.bfloat16
CHUNK = 512


def prepare_kernel(acts, gain, first, out):
    wide = acts[...].astype(F32)
    scale = lax.rsqrt(jnp.mean(wide * wide, axis=-1, keepdims=True) + 1e-05)
    normed = (wide * scale * gain[...]).astype(BF16)
    lanes = lax.broadcasted_iota(jnp.int32, (acts.shape[0], 128), 1)
    for to in range(RING):
        out[to, :, :2048] = normed
        at = to // 2 * 128
        low = first[:, at : at + 128].astype(F32)
        high = first[:, 256 + at : 384 + at].astype(F32)
        if to % 2 == 0:
            high = pltpu.roll(high, 64, 1)
        else:
            low = pltpu.roll(low, 64, 1)
        out[to, :, 2048:] = jnp.where(lanes < 64, low, high).astype(BF16)


def pull(x, axis, by):
    n = lax.axis_size(axis)
    return lax.ppermute(x, axis, [((i + by) % n, i) for i in range(n)])


def rope_tables(positions, head_dim):
    half = head_dim // 2
    freq = rope_base ** (-2.0 * jnp.arange(half, dtype=F32) / head_dim)
    angle = positions.astype(F32)[:, None] * freq
    cosine, sine = jnp.cos(angle), jnp.sin(angle)
    return (
        jnp.concatenate([cosine] * 4, axis=-1),
        jnp.concatenate([-sine, sine, -sine, sine], axis=-1),
    )


def rope(u, cosine, sine):
    lanes = lax.broadcasted_iota(jnp.int32, u.shape, 1)
    swapped = jnp.where(lanes % 64 < 32, pltpu.roll(u, 96, 1), pltpu.roll(u, 32, 1))
    return u * cosine + swapped * sine


def keyval_kernel(place, x, mine, theirs, cos, sin, mix, *refs):
    kv_out, val_out, w = refs[-3:]
    h, c, section = place[1], place[2], place[3]
    w[0:64], w[64:128], w[128:192], w[192:256] = mine[0:64], theirs[0:64], mine[64:128], theirs[64:128]
    both = lax.dot_general(x[:, :2048], w[...], (((1,), (1,)), ((), ())), preferred_element_type=F32)
    rows = 128
    for slot in range(RING):
        part = both[slot * rows : (slot + 1) * rows]
        own, other = part[:, :128], part[:, 128:]
        keys = jnp.where(h == 0, own, other)
        values = jnp.where(h == 0, other, own)
        keys = jnp.where(c == 0, keys, pltpu.roll(keys, 64, 1))
        values = jnp.where(c == 0, values, pltpu.roll(values, 64, 1))
        rounded = values.astype(BF16)
        wide = rounded.astype(F32)
        before = jnp.where(section == 0, wide, x[slot * rows : (slot + 1) * rows, 2048:].astype(F32))
        mixed = mix[0:1, :] * wide + (1.0 - mix[0:1, :]) * before
        keys = rope(keys, cos[slot], sin[slot])
        lanes = lax.broadcasted_iota(jnp.int32, keys.shape, 1)
        low = jnp.where(lanes < 64, keys, pltpu.roll(mixed, 64, 1))
        high = jnp.where(lanes < 64, pltpu.roll(keys, 64, 1), mixed)
        kv_out[slot, :, 0:128] = low.astype(BF16)
        kv_out[slot, :, 128:256] = high.astype(BF16)
        val_out[slot] = rounded


def bundle_kernel(w_q, w_o, out):
    out[0] = w_q[...]
    for k in range(4):
        out[1, k * 128 : (k + 1) * 128, :] = w_o[:, k * 128 : (k + 1) * 128]


def query_kernel(x, wa, wb, cos, sin, out, w):
    w[:, :128], w[:, 128:] = wa[:2048], wb[:2048]
    both = jnp.dot(x[:, :2048], w[...], preferred_element_type=F32)
    for slot in range(RING):
        part = both[slot * 128 : (slot + 1) * 128]
        for pair in range(2):
            u = rope(part[:, pair * 128 : (pair + 1) * 128], cos[slot], sin[slot])
            out[slot, :, pair * 128 : (pair + 1) * 128] = (u * 0.125).astype(BF16)


def attend_kernel(place, q, kv, kv_c, before, before_c, *refs):
    out, keys, vals, scores, q4 = refs[-5:]
    step = pl.program_id(0)
    h, c = place[1], place[2]
    lanes = lax.broadcasted_iota(jnp.int32, (128, 128), 1)

    def place_block(src, k, half, core):
        both = src[k].astype(F32)
        turned = pltpu.roll(both, 64, 1)
        at = pl.ds(pl.multiple_of(half * 1024 + k * 256 + core * 128, 128), 128)
        keys[:, at] = jnp.where(lanes < 64, both, turned).T.astype(BF16)
        vals[at, :] = jnp.where(lanes < 64, turned, 1.0).astype(BF16)

    @pl.when(step == 0)
    def _():
        for k in range(RING):
            place_block(kv, k, h, c)
            place_block(kv_c, k, h, 1 - c)

    @pl.when((step == 0) & (h == 1))
    def _():
        for k in range(RING):
            place_block(before, k, 0, c)
            place_block(before_c, k, 0, 1 - c)

    for pair in range(2):
        block = q[0, :, pair * 128 : (pair + 1) * 128].astype(F32)
        q4[pair * 256 : pair * 256 + 128] = jnp.where(lanes < 64, block, 0.0).astype(BF16)
        q4[pair * 256 + 128 : pair * 256 + 256] = jnp.where(lanes < 64, 0.0, block).astype(BF16)
    last = h * (1024 // CHUNK) + step * 256 // CHUNK

    def dots(j):
        chunk = keys[:, pl.ds(pl.multiple_of(j * CHUNK, CHUNK), CHUNK)]
        return jnp.dot(q4[...], chunk, preferred_element_type=F32)

    def greatest(s):
        top = s[:, :128]
        for k in range(1, CHUNK // 128):
            top = jnp.maximum(top, s[:, k * 128 : (k + 1) * 128])
        return top

    s = dots(last)
    row = lax.rem(lax.broadcasted_iota(jnp.int32, s.shape, 0), 128) + c * 128 + lax.rem(step * 256, CHUNK)
    col = lax.broadcasted_iota(jnp.int32, s.shape, 1)
    s = jnp.where(col <= row, s, -1e30)
    scores[last] = s

    def first_pass(j, top):
        s = dots(j)
        scores[j] = s
        return jnp.maximum(top, greatest(s))

    top = lax.fori_loop(0, last, first_pass, greatest(s))
    top = jnp.max(top, axis=1, keepdims=True)

    def second_pass(j, acc):
        p = jnp.exp(scores[j] - top).astype(BF16)
        chunk = vals[pl.ds(pl.multiple_of(j * CHUNK, CHUNK), CHUNK), :]
        return acc + jnp.dot(p, chunk, preferred_element_type=F32)

    acc = lax.fori_loop(0, last + 1, second_pass, jnp.zeros((512, 128), F32))
    result = acc / pltpu.roll(acc, 64, 1)
    for pair in range(2):
        left = result[pair * 256 : pair * 256 + 128]
        right = pltpu.roll(result[pair * 256 + 128 : pair * 256 + 256], 64, 1)
        out[0, :, pair * 128 : (pair + 1) * 128] = jnp.where(lanes < 64, left, right).astype(BF16)


def gather_heads_kernel(place, parts, out):
    lanes = lax.broadcasted_iota(jnp.int32, (128, 128), 1)
    keep = jnp.where(place[3] == 0, 1.0, 0.0)
    for k in range(0, RING, 2):
        left, right = parts[k].astype(F32) * keep, parts[k + 1].astype(F32) * keep
        at = k // 2 * 128
        out[:, at : at + 128] = jnp.where(lanes < 64, left, pltpu.roll(right, 64, 1)).astype(BF16)
        out[:, 256 + at : 384 + at] = jnp.where(lanes < 64, pltpu.roll(left, 64, 1), right).astype(BF16)


def times_rows(att, wa, wb, w):
    for half, pieces in enumerate((wa, wb)):
        at = 0
        for piece, begin in pieces:
            for row in range(begin, piece.shape[0], 128):
                w[half * 128 : half * 128 + 128, at : at + 128] = piece[row : row + 128, :]
                at += 128
    return jnp.dot(att.reshape(256, 256), w[...], preferred_element_type=F32)


def out_own_kernel(near, far, qo, qo_c, z1, z1c, z2, z2c, total, w):
    total[...] = times_rows(near[0:2], [(qo, 2048)], [(qo_c, 2048)], w)
    total[...] += times_rows(far[0:2], [(z1, 2048), (z2, 0)], [(z1c, 2048), (z2c, 0)], w)


def out_beside_kernel(place, acts, base, near, far, o_b, o_bc, o_zb, o_zbc, fresh, mine, theirs, w):
    odd = lax.rem(place[0], 2)
    total = base[...] + times_rows(near[...], [(o_b, 0)], [(o_bc, 0)], w)
    total += times_rows(far[...], [(o_zb, 0)], [(o_zbc, 0)], w)
    low, high = total[:128], total[128:]
    mine[...] = (acts[...].astype(F32) + jnp.where(odd == 0, low, high)).astype(BF16)
    theirs[...] = jnp.where(odd == 0, high, low).astype(BF16)


def params(mib):
    return pltpu.CompilerParams(vmem_limit_bytes=mib * 2**20)


VM = pl.BlockSpec(memory_space=pltpu.VMEM)
SM = pl.BlockSpec(memory_space=pltpu.SMEM)


def prepare(acts, gain, first):
    return pl.pallas_call(
        prepare_kernel,
        out_shape=jax.ShapeDtypeStruct((RING, acts.shape[0], 2048 + 128), BF16),
        grid=(4,),
        in_specs=[
            pl.BlockSpec((32, 2048), lambda i: (i, 0)),
            pl.BlockSpec((1, 2048), lambda i: (0, 0)),
            pl.BlockSpec((32, 512), lambda i: (i, 0)),
        ],
        out_specs=pl.BlockSpec((RING, 32, 2048 + 128), lambda i: (0, i, 0)),
        compiler_params=params(16),
        cost_estimate=pl.CostEstimate(flops=2 * 512 * 2048 * 256, bytes_accessed=4 << 20, transcendentals=0),
    )(acts, gain, first)


def keyval(operands, *others):
    return pl.pallas_call(
        keyval_kernel,
        out_shape=(jax.ShapeDtypeStruct((4, 128, 256), BF16), jax.ShapeDtypeStruct((4, 128, 128), BF16)),
        in_specs=[SM] + [VM] * 6 + [pl.BlockSpec(memory_space=pl.ANY)] * len(others),
        out_specs=(VM, VM),
        scratch_shapes=[pltpu.VMEM((256, 2048), BF16)],
        compiler_params=params(24),
        cost_estimate=pl.CostEstimate(flops=2 * 512 * 2048 * 256, bytes_accessed=4 << 20, transcendentals=0),
    )(*operands, *others)


def query(x, wa, wb, cos, sin):
    return pl.pallas_call(
        query_kernel,
        out_shape=jax.ShapeDtypeStruct((4, 128, 256), BF16),
        in_specs=[VM] * 5,
        out_specs=VM,
        scratch_shapes=[pltpu.VMEM((2048, 256), BF16)],
        compiler_params=params(24),
        cost_estimate=pl.CostEstimate(flops=2 * 512 * 2048 * 256, bytes_accessed=4 << 20, transcendentals=0),
    )(x, wa, wb, cos, sin)


def attend(place, q, kvs, *others):
    def at(step, place):
        return (step, 0, 0)

    def to(step, place):
        return (lax.rem(step + place[0] // 2 * 2, RING), 0, 0)

    return pl.pallas_call(
        attend_kernel,
        out_shape=jax.ShapeDtypeStruct((4, 128, 256), BF16),
        grid_spec=pltpu.PrefetchScalarGridSpec(
            num_scalar_prefetch=1,
            grid=(RING,),
            in_specs=[
                pl.BlockSpec((1, 128, 256), at),
            ]
            + [pl.BlockSpec((RING, 128, 128), lambda step, place: (0, 0, place[4]))] * 4
            + [pl.BlockSpec(memory_space=pl.ANY)] * len(others),
            out_specs=pl.BlockSpec((1, 128, 256), to),
            scratch_shapes=[
                pltpu.VMEM((128, 2048), BF16),
                pltpu.VMEM((2048, 128), BF16),
                pltpu.VMEM((2048 // CHUNK, 512, CHUNK), F32),
                pltpu.VMEM((512, 128), BF16),
            ],
        ),
        compiler_params=params(24),
        cost_estimate=pl.CostEstimate(flops=2 * 2 * 512 * 256 * 6656, bytes_accessed=32 << 20, transcendentals=512 * 6656),
    )(place, q, *kvs, *others)


def bundle(w_q, w_o):
    return pl.pallas_call(
        bundle_kernel,
        out_shape=jax.ShapeDtypeStruct((2, 2048, 128), BF16),
        grid=(4,),
        in_specs=[pl.BlockSpec((512, 128), lambda i: (i, 0)), pl.BlockSpec((128, 512), lambda i: (0, i))],
        out_specs=pl.BlockSpec((2, 512, 128), lambda i: (0, i, 0)),
        compiler_params=params(16),
        cost_estimate=pl.CostEstimate(flops=0, bytes_accessed=2 << 20, transcendentals=0),
    )(w_q, w_o)


def out_own(*operands):
    return pl.pallas_call(
        out_own_kernel,
        out_shape=jax.ShapeDtypeStruct((256, 2048), F32),
        in_specs=[VM] * 8,
        out_specs=VM,
        scratch_shapes=[pltpu.VMEM((256, 2048), BF16)],
        compiler_params=params(32),
        cost_estimate=pl.CostEstimate(flops=2 * 256 * 512 * 2048, bytes_accessed=4 << 20, transcendentals=0),
    )(*operands)


def out_beside(*operands):
    return pl.pallas_call(
        out_beside_kernel,
        out_shape=(jax.ShapeDtypeStruct((128, 2048), BF16),) * 2,
        in_specs=[SM] + [VM] * 8 + [pl.BlockSpec(memory_space=pl.ANY)],
        out_specs=(VM, VM),
        scratch_shapes=[pltpu.VMEM((256, 2048), BF16)],
        compiler_params=params(32),
        cost_estimate=pl.CostEstimate(flops=2 * 256 * 512 * 2048, bytes_accessed=4 << 20, transcendentals=0),
    )(*operands)


def hold(arrays, *others):
    n = len(arrays)
    return pl.pallas_call(
        lambda *refs: None,
        out_shape=[jax.ShapeDtypeStruct(x.shape, x.dtype) for x in arrays],
        in_specs=[pl.BlockSpec(memory_space=pl.ANY)] * (n + len(others)),
        out_specs=[pl.BlockSpec(memory_space=pl.ANY)] * n,
        input_output_aliases={k: k for k in range(n)},
    )(*arrays, *others)


def gather_heads(place, parts):
    return pl.pallas_call(
        gather_heads_kernel,
        out_shape=jax.ShapeDtypeStruct((128, 512), BF16),
        in_specs=[SM, VM],
        out_specs=VM,
        cost_estimate=pl.CostEstimate(flops=0, bytes_accessed=1 << 18, transcendentals=0),
    )(place, parts)


def beside_b(x):
    return lax.ppermute(x, "y", [(y, RING - 1 - y) for y in range(RING)])


def swap(x):
    return lax.all_to_all(x, "y", 0, 0)


def per_device(acts, norm_gain, query_weight, kv_weight, out_weight, first_values, mix_weight):
    inputs = acts[0]
    tok = inputs.shape[0]
    h, y, c = lax.axis_index("zh"), lax.axis_index("y"), lax.axis_index("c")
    section = lax.axis_index("x") * ZS + lax.axis_index("zl")
    place = jnp.stack([y, h, c, section, h]).astype(jnp.int32)
    place_far = jnp.stack([y, h, c, section, 1 - h]).astype(jnp.int32)
    core = functools.partial(pull, axis="c", by=1)
    half = functools.partial(pull, axis="zh", by=1)

    positions = h * 8 * tok + (2 * jnp.arange(RING, dtype=jnp.int32)[:, None] + c) * tok + jnp.arange(tok, dtype=jnp.int32)
    cos, sin = (t.reshape(RING, tok, 128) for t in rope_tables(positions.reshape(-1), 64))
    mix_two = lax.dynamic_index_in_dim(mix_weight[0].reshape(2, RING), y, 1, keepdims=False)
    mix = jnp.broadcast_to(jnp.repeat(mix_two, 64)[None, :], (8, 128))

    x = swap(prepare(inputs, norm_gain, first_values[0]))

    w_kv = kv_weight[0].T
    home = [(s, s // 8 * 8 + s % 4 * 2 + s % 8 // 4) for s in range(16)]
    kv_b = lax.ppermute(w_kv, SEQ, [(s, (d + 8) % 16) for s, d in home])
    kv_a = lax.ppermute(w_kv, SEQ, home)
    mine = jnp.concatenate([kv_a, kv_b], axis=0)
    theirs = core(mine)

    qo = bundle(query_weight[0], out_weight[0])
    qo = qo.reshape(4096, 128)
    z1, qo_c = half(qo[:3072]), core(qo)
    x = x.reshape(RING * tok, 2048 + 128)
    kv, values = keyval((place, x, mine, theirs, cos, sin, mix))

    kv_c = core(kv)
    kv_before = lax.ppermute(kv, "zh", [(0, 1)])
    q_near = query(x, qo, qo_c, cos, sin)
    fresh = gather_heads(place, swap(values))
    kv_before, o_2 = hold([kv_before, qo[3072:]], q_near, fresh)
    kv_before_c = core(kv_before)
    kvs = (kv, kv_c, kv_before, kv_before_c)

    kv_before, o_2 = hold([kv_before, qo[3072:]], q_near, fresh)
    kv_before_c = core(kv_before)
    kvs = (kv, kv_c, kv_before, kv_before_c)

    def sent_on(x, stride):
        return [lax.ppermute(x, PIPE, [(p, p + k * stride) for p in range(stride)]) for k in range(1, 4)]

    def sent_on(x, *rounds):
        return sum([lax.ppermute(x, PIPE, pairs) for pairs in rounds], x)

    z1, o_own, fresh = hold([z1, qo[2048:], fresh], kv_before_c)
    fresh = sent_on(fresh, [(0, 2)])
    z2 = half(o_2)
    o_b = beside_b(o_own)
    att_near = attend(place, q_near, kvs)
    z1c = core(z1)
    q_far = query(x, z1, z1c, cos, sin)

    q_far, z2, o_b, fresh = hold([q_far, z2, o_b, fresh], att_near)
    fresh = sent_on(fresh, [(0, 1), (2, 3)])
    att_far = attend(place_far, q_far, kvs)
    o_zb = beside_b(jnp.concatenate([z1[2048:], z2], axis=0))
    near = beside_b(att_near[2:4])
    z2c, o_bc = core(z2), core(o_b)

    o_zb, fresh = hold([o_zb, fresh], att_far, near, z2c, o_bc)
    far = beside_b(att_far[2:4])
    o_zbc = core(o_zb)
    fresh = sent_on(fresh, *[[(p, p + k * ZS) for p in range(ZS)] for k in range(1, XS)])
    total = out_own(att_near, att_far, qo, qo_c, z1, z1c, z2, z2c)
    mine, theirs = out_beside(place, inputs, total, near, far, o_b, o_bc, o_zb, o_zbc, fresh)

    onward = [(p, (p + 1) % (XS * ZS)) for p in range(XS * ZS)]
    across = [(y * XS * ZS + p, (y ^ 1) * XS * ZS + q) for p, q in onward for y in range(RING)]
    sums = [lax.ppermute(theirs, ("y",) + PIPE, across), lax.ppermute(mine, PIPE, onward)]
    passed = (sums[0].astype(F32) + sums[1].astype(F32)).astype(BF16)
    return (passed[None], fresh[None])


def solution(mesh):
    split = Mesh(mesh.devices.reshape(HALVES, RING, CORES, XS, ZS), SEQ + PIPE)
    placed = (
        P(PIPE, SEQ, None),
        P(PIPE, None),
        P(PIPE, None, SEQ),
        P(PIPE, None, SEQ),
        P(PIPE, SEQ, None),
        P(PIPE, SEQ, None),
        P(PIPE, None),
    )
    return jax.shard_map(
        per_device,
        mesh=split,
        in_specs=placed,
        out_specs=(P(PIPE, SEQ, None), P(PIPE, SEQ, None)),
        check_vma=False,
    )
```

```python
import functools

import jax
import jax.numpy as jnp
from jax import lax
from jax.experimental import pallas as pl
from jax.experimental.pallas import tpu as pltpu
from jax.sharding import Mesh
from jax.sharding import PartitionSpec as P

HALVES, RING, CORES, XS, ZS = 2, 4, 2, 4, 4
SEQ = ("zh", "y", "c")
PIPE = ("x", "zl")
rope_base = 500000.0
F32 = jnp.float32
BF16 = jnp.bfloat16
CHUNK = 512


def prepare_kernel(acts, gain, first, out):
    wide = acts[...].astype(F32)
    scale = lax.rsqrt(jnp.mean(wide * wide, axis=-1, keepdims=True) + 1e-05)
    normed = (wide * scale * gain[...]).astype(BF16)
    lanes = lax.broadcasted_iota(jnp.int32, (acts.shape[0], 128), 1)
    for to in range(RING):
        out[to, :, :2048] = normed
        at = to // 2 * 128
        low = first[:, at : at + 128].astype(F32)
        high = first[:, 256 + at : 384 + at].astype(F32)
        if to % 2 == 0:
            high = pltpu.roll(high, 64, 1)
        else:
            low = pltpu.roll(low, 64, 1)
        out[to, :, 2048:] = jnp.where(lanes < 64, low, high).astype(BF16)


def pull(x, axis, by):
    n = lax.axis_size(axis)
    return lax.ppermute(x, axis, [((i + by) % n, i) for i in range(n)])


def rope_tables(positions, head_dim):
    half = head_dim // 2
    freq = rope_base ** (-2.0 * jnp.arange(half, dtype=F32) / head_dim)
    angle = positions.astype(F32)[:, None] * freq
    cosine, sine = jnp.cos(angle), jnp.sin(angle)
    return (
        jnp.concatenate([cosine] * 4, axis=-1),
        jnp.concatenate([-sine, sine, -sine, sine], axis=-1),
    )


def rope(u, cosine, sine):
    lanes = lax.broadcasted_iota(jnp.int32, u.shape, 1)
    swapped = jnp.where(lanes % 64 < 32, pltpu.roll(u, 96, 1), pltpu.roll(u, 32, 1))
    return u * cosine + swapped * sine


def keyval_kernel(place, x, mine, theirs, cos, sin, mix, *refs):
    kv_out, val_out, w = refs[-3:]
    h, c, section = place[1], place[2], place[3]
    w[0:64], w[64:128], w[128:192], w[192:256] = mine[0:64], theirs[0:64], mine[64:128], theirs[64:128]
    both = lax.dot_general(x[:, :2048], w[...], (((1,), (1,)), ((), ())), preferred_element_type=F32)
    rows = 128
    for slot in range(RING):
        part = both[slot * rows : (slot + 1) * rows]
        own, other = part[:, :128], part[:, 128:]
        keys = jnp.where(h == 0, own, other)
        values = jnp.where(h == 0, other, own)
        keys = jnp.where(c == 0, keys, pltpu.roll(keys, 64, 1))
        values = jnp.where(c == 0, values, pltpu.roll(values, 64, 1))
        rounded = values.astype(BF16)
        wide = rounded.astype(F32)
        before = jnp.where(section == 0, wide, x[slot * rows : (slot + 1) * rows, 2048:].astype(F32))
        mixed = mix[0:1, :] * wide + (1.0 - mix[0:1, :]) * before
        keys = rope(keys, cos[slot], sin[slot])
        lanes = lax.broadcasted_iota(jnp.int32, keys.shape, 1)
        low = jnp.where(lanes < 64, keys, pltpu.roll(mixed, 64, 1))
        high = jnp.where(lanes < 64, pltpu.roll(keys, 64, 1), mixed)
        kv_out[slot, :, 0:128] = low.astype(BF16)
        kv_out[slot, :, 128:256] = high.astype(BF16)
        val_out[slot] = rounded


def bundle_kernel(w_q, w_o, out):
    out[0] = w_q[...]
    for k in range(4):
        out[1, k * 128 : (k + 1) * 128, :] = w_o[:, k * 128 : (k + 1) * 128]


def query_kernel(x, wa, wb, cos, sin, out, w):
    w[:, :128], w[:, 128:] = wa[:2048], wb[:2048]
    both = jnp.dot(x[:, :2048], w[...], preferred_element_type=F32)
    for slot in range(RING):
        part = both[slot * 128 : (slot + 1) * 128]
        for pair in range(2):
            u = rope(part[:, pair * 128 : (pair + 1) * 128], cos[slot], sin[slot])
            out[slot, :, pair * 128 : (pair + 1) * 128] = (u * 0.125).astype(BF16)


def attend_kernel(place, q, kv, kv_c, before, before_c, *refs):
    out, keys, vals, scores, q4 = refs[-5:]
    step = pl.program_id(0)
    h, c = place[1], place[2]
    lanes = lax.broadcasted_iota(jnp.int32, (128, 128), 1)

    def place_block(src, k, half, core):
        both = src[k].astype(F32)
        turned = pltpu.roll(both, 64, 1)
        at = pl.ds(pl.multiple_of(half * 1024 + k * 256 + core * 128, 128), 128)
        keys[:, at] = jnp.where(lanes < 64, both, turned).T.astype(BF16)
        vals[at, :] = jnp.where(lanes < 64, turned, 1.0).astype(BF16)

    @pl.when(step == 0)
    def _():
        for k in range(RING):
            place_block(kv, k, h, c)
            place_block(kv_c, k, h, 1 - c)

    @pl.when((step == 0) & (h == 1))
    def _():
        for k in range(RING):
            place_block(before, k, 0, c)
            place_block(before_c, k, 0, 1 - c)

    for pair in range(2):
        block = q[0, :, pair * 128 : (pair + 1) * 128].astype(F32)
        q4[pair * 256 : pair * 256 + 128] = jnp.where(lanes < 64, block, 0.0).astype(BF16)
        q4[pair * 256 + 128 : pair * 256 + 256] = jnp.where(lanes < 64, 0.0, block).astype(BF16)
    last = h * (1024 // CHUNK) + step * 256 // CHUNK

    def dots(j):
        chunk = keys[:, pl.ds(pl.multiple_of(j * CHUNK, CHUNK), CHUNK)]
        return jnp.dot(q4[...], chunk, preferred_element_type=F32)

    def greatest(s):
        top = s[:, :128]
        for k in range(1, CHUNK // 128):
            top = jnp.maximum(top, s[:, k * 128 : (k + 1) * 128])
        return top

    s = dots(last)
    row = lax.rem(lax.broadcasted_iota(jnp.int32, s.shape, 0), 128) + c * 128 + lax.rem(step * 256, CHUNK)
    col = lax.broadcasted_iota(jnp.int32, s.shape, 1)
    s = jnp.where(col <= row, s, -1e30)
    scores[last] = s

    def first_pass(j, top):
        s = dots(j)
        scores[j] = s
        return jnp.maximum(top, greatest(s))

    top = lax.fori_loop(0, last, first_pass, greatest(s))
    top = jnp.max(top, axis=1, keepdims=True)

    def second_pass(j, acc):
        p = jnp.exp(scores[j] - top).astype(BF16)
        chunk = vals[pl.ds(pl.multiple_of(j * CHUNK, CHUNK), CHUNK), :]
        return acc + jnp.dot(p, chunk, preferred_element_type=F32)

    acc = lax.fori_loop(0, last + 1, second_pass, jnp.zeros((512, 128), F32))
    result = acc / pltpu.roll(acc, 64, 1)
    for pair in range(2):
        left = result[pair * 256 : pair * 256 + 128]
        right = pltpu.roll(result[pair * 256 + 128 : pair * 256 + 256], 64, 1)
        out[0, :, pair * 128 : (pair + 1) * 128] = jnp.where(lanes < 64, left, right).astype(BF16)


def gather_heads_kernel(place, parts, out):
    lanes = lax.broadcasted_iota(jnp.int32, (128, 128), 1)
    keep = jnp.where(place[3] == 0, 1.0, 0.0)
    for k in range(0, RING, 2):
        left, right = parts[k].astype(F32) * keep, parts[k + 1].astype(F32) * keep
        at = k // 2 * 128
        out[:, at : at + 128] = jnp.where(lanes < 64, left, pltpu.roll(right, 64, 1)).astype(BF16)
        out[:, 256 + at : 384 + at] = jnp.where(lanes < 64, pltpu.roll(left, 64, 1), right).astype(BF16)


def times_rows(att, wa, wb, w):
    for half, pieces in enumerate((wa, wb)):
        at = 0
        for piece, begin in pieces:
            for row in range(begin, piece.shape[0], 128):
                w[half * 128 : half * 128 + 128, at : at + 128] = piece[row : row + 128, :]
                at += 128
    return jnp.dot(att.reshape(256, 256), w[...], preferred_element_type=F32)


def out_own_kernel(near, far, qo, qo_c, z1, z1c, z2, z2c, total, w):
    total[...] = times_rows(near[0:2], [(qo, 2048)], [(qo_c, 2048)], w)
    total[...] += times_rows(far[0:2], [(z1, 2048), (z2, 0)], [(z1c, 2048), (z2c, 0)], w)


def out_beside_kernel(place, acts, base, near, far, o_b, o_bc, o_zb, o_zbc, fresh, mine, theirs, w):
    odd = lax.rem(place[0], 2)
    total = base[...] + times_rows(near[...], [(o_b, 0)], [(o_bc, 0)], w)
    total += times_rows(far[...], [(o_zb, 0)], [(o_zbc, 0)], w)
    low, high = total[:128], total[128:]
    mine[...] = (acts[...].astype(F32) + jnp.where(odd == 0, low, high)).astype(BF16)
    theirs[...] = jnp.where(odd == 0, high, low).astype(BF16)


def params(mib):
    return pltpu.CompilerParams(vmem_limit_bytes=mib * 2**20)


VM = pl.BlockSpec(memory_space=pltpu.VMEM)
SM = pl.BlockSpec(memory_space=pltpu.SMEM)


def prepare(acts, gain, first):
    return pl.pallas_call(
        prepare_kernel,
        out_shape=jax.ShapeDtypeStruct((RING, acts.shape[0], 2048 + 128), BF16),
        grid=(4,),
        in_specs=[
            pl.BlockSpec((32, 2048), lambda i: (i, 0)),
            pl.BlockSpec((1, 2048), lambda i: (0, 0)),
            pl.BlockSpec((32, 512), lambda i: (i, 0)),
        ],
        out_specs=pl.BlockSpec((RING, 32, 2048 + 128), lambda i: (0, i, 0)),
        compiler_params=params(16),
        cost_estimate=pl.CostEstimate(flops=2 * 512 * 2048 * 256, bytes_accessed=4 << 20, transcendentals=0),
    )(acts, gain, first)


def keyval(operands, *others):
    return pl.pallas_call(
        keyval_kernel,
        out_shape=(jax.ShapeDtypeStruct((4, 128, 256), BF16), jax.ShapeDtypeStruct((4, 128, 128), BF16)),
        in_specs=[SM] + [VM] * 6 + [pl.BlockSpec(memory_space=pl.ANY)] * len(others),
        out_specs=(VM, VM),
        scratch_shapes=[pltpu.VMEM((256, 2048), BF16)],
        compiler_params=params(24),
        cost_estimate=pl.CostEstimate(flops=2 * 512 * 2048 * 256, bytes_accessed=4 << 20, transcendentals=0),
    )(*operands, *others)


def query(x, wa, wb, cos, sin):
    return pl.pallas_call(
        query_kernel,
        out_shape=jax.ShapeDtypeStruct((4, 128, 256), BF16),
        in_specs=[VM] * 5,
        out_specs=VM,
        scratch_shapes=[pltpu.VMEM((2048, 256), BF16)],
        compiler_params=params(24),
        cost_estimate=pl.CostEstimate(flops=2 * 512 * 2048 * 256, bytes_accessed=4 << 20, transcendentals=0),
    )(x, wa, wb, cos, sin)


def attend(place, q, kvs, *others):
    def at(step, place):
        return (step, 0, 0)

    def to(step, place):
        return (lax.rem(step + place[0] // 2 * 2, RING), 0, 0)

    return pl.pallas_call(
        attend_kernel,
        out_shape=jax.ShapeDtypeStruct((4, 128, 256), BF16),
        grid_spec=pltpu.PrefetchScalarGridSpec(
            num_scalar_prefetch=1,
            grid=(RING,),
            in_specs=[
                pl.BlockSpec((1, 128, 256), at),
            ]
            + [pl.BlockSpec((RING, 128, 128), lambda step, place: (0, 0, place[4]))] * 4
            + [pl.BlockSpec(memory_space=pl.ANY)] * len(others),
            out_specs=pl.BlockSpec((1, 128, 256), to),
            scratch_shapes=[
                pltpu.VMEM((128, 2048), BF16),
                pltpu.VMEM((2048, 128), BF16),
                pltpu.VMEM((2048 // CHUNK, 512, CHUNK), F32),
                pltpu.VMEM((512, 128), BF16),
            ],
        ),
        compiler_params=params(24),
        cost_estimate=pl.CostEstimate(flops=2 * 2 * 512 * 256 * 6656, bytes_accessed=32 << 20, transcendentals=512 * 6656),
    )(place, q, *kvs, *others)


def bundle(w_q, w_o):
    return pl.pallas_call(
        bundle_kernel,
        out_shape=jax.ShapeDtypeStruct((2, 2048, 128), BF16),
        grid=(4,),
        in_specs=[pl.BlockSpec((512, 128), lambda i: (i, 0)), pl.BlockSpec((128, 512), lambda i: (0, i))],
        out_specs=pl.BlockSpec((2, 512, 128), lambda i: (0, i, 0)),
        compiler_params=params(16),
        cost_estimate=pl.CostEstimate(flops=0, bytes_accessed=2 << 20, transcendentals=0),
    )(w_q, w_o)


def out_own(*operands):
    return pl.pallas_call(
        out_own_kernel,
        out_shape=jax.ShapeDtypeStruct((256, 2048), F32),
        in_specs=[VM] * 8,
        out_specs=VM,
        scratch_shapes=[pltpu.VMEM((256, 2048), BF16)],
        compiler_params=params(32),
        cost_estimate=pl.CostEstimate(flops=2 * 256 * 512 * 2048, bytes_accessed=4 << 20, transcendentals=0),
    )(*operands)


def out_beside(*operands):
    return pl.pallas_call(
        out_beside_kernel,
        out_shape=(jax.ShapeDtypeStruct((128, 2048), BF16),) * 2,
        in_specs=[SM] + [VM] * 8 + [pl.BlockSpec(memory_space=pl.ANY)],
        out_specs=(VM, VM),
        scratch_shapes=[pltpu.VMEM((256, 2048), BF16)],
        compiler_params=params(32),
        cost_estimate=pl.CostEstimate(flops=2 * 256 * 512 * 2048, bytes_accessed=4 << 20, transcendentals=0),
    )(*operands)


def hold(arrays, *others):
    n = len(arrays)
    return pl.pallas_call(
        lambda *refs: None,
        out_shape=[jax.ShapeDtypeStruct(x.shape, x.dtype) for x in arrays],
        in_specs=[pl.BlockSpec(memory_space=pl.ANY)] * (n + len(others)),
        out_specs=[pl.BlockSpec(memory_space=pl.ANY)] * n,
        input_output_aliases={k: k for k in range(n)},
    )(*arrays, *others)


def gather_heads(place, parts):
    return pl.pallas_call(
        gather_heads_kernel,
        out_shape=jax.ShapeDtypeStruct((128, 512), BF16),
        in_specs=[SM, VM],
        out_specs=VM,
        cost_estimate=pl.CostEstimate(flops=0, bytes_accessed=1 << 18, transcendentals=0),
    )(place, parts)


def beside_b(x):
    return lax.ppermute(x, "y", [(y, RING - 1 - y) for y in range(RING)])


def swap(x):
    return lax.all_to_all(x, "y", 0, 0)


def per_device(acts, norm_gain, query_weight, kv_weight, out_weight, first_values, mix_weight):
    inputs = acts[0]
    tok = inputs.shape[0]
    h, y, c = lax.axis_index("zh"), lax.axis_index("y"), lax.axis_index("c")
    section = lax.axis_index("x") * ZS + lax.axis_index("zl")
    place = jnp.stack([y, h, c, section, h]).astype(jnp.int32)
    place_far = jnp.stack([y, h, c, section, 1 - h]).astype(jnp.int32)
    core = functools.partial(pull, axis="c", by=1)
    half = functools.partial(pull, axis="zh", by=1)

    positions = h * 8 * tok + (2 * jnp.arange(RING, dtype=jnp.int32)[:, None] + c) * tok + jnp.arange(tok, dtype=jnp.int32)
    cos, sin = (t.reshape(RING, tok, 128) for t in rope_tables(positions.reshape(-1), 64))
    mix_two = lax.dynamic_index_in_dim(mix_weight[0].reshape(2, RING), y, 1, keepdims=False)
    mix = jnp.broadcast_to(jnp.repeat(mix_two, 64)[None, :], (8, 128))

    x = swap(prepare(inputs, norm_gain, first_values[0]))

    w_kv = kv_weight[0].T
    home = [(s, s // 8 * 8 + s % 4 * 2 + s % 8 // 4) for s in range(16)]
    kv_b = lax.ppermute(w_kv, SEQ, [(s, (d + 8) % 16) for s, d in home])
    kv_a = lax.ppermute(w_kv, SEQ, home)
    mine = jnp.concatenate([kv_a, kv_b], axis=0)
    theirs = core(mine)

    qo = bundle(query_weight[0], out_weight[0])
    qo = qo.reshape(4096, 128)
    z1, qo_c = half(qo[:3072]), core(qo)
    x = x.reshape(RING * tok, 2048 + 128)
    kv, values = keyval((place, x, mine, theirs, cos, sin, mix))

    kv_c = core(kv)
    kv_before = lax.ppermute(kv, "zh", [(0, 1)])
    q_near = query(x, qo, qo_c, cos, sin)
    fresh = gather_heads(place, swap(values))
    kv_before, o_2 = hold([kv_before, qo[3072:]], q_near, fresh)
    kv_before_c = core(kv_before)
    kvs = (kv, kv_c, kv_before, kv_before_c)

    kv_before, o_2 = hold([kv_before, qo[3072:]], q_near, fresh)
    kv_before_c = core(kv_before)
    kvs = (kv, kv_c, kv_before, kv_before_c)

    def sent_on(x, stride):
        return [lax.ppermute(x, PIPE, [(p, p + k * stride) for p in range(stride)]) for k in range(1, 4)]

    def sent_on(x, by):
        return x + lax.ppermute(x, PIPE, [(p, p + by) for p in range(0, XS * ZS, 2 * by)])

    fresh = sent_on(fresh, 8)

    z1, o_own, fresh = hold([z1, qo[2048:], fresh], kv_before_c)
    fresh = sent_on(fresh, 4)
    z2 = half(o_2)
    o_b = beside_b(o_own)
    att_near = attend(place, q_near, kvs)
    z1c = core(z1)
    q_far = query(x, z1, z1c, cos, sin)

    q_far, z2, o_b, fresh = hold([q_far, z2, o_b, fresh], att_near)
    fresh = sent_on(fresh, 2)
    att_far = attend(place_far, q_far, kvs)
    o_zb = beside_b(jnp.concatenate([z1[2048:], z2], axis=0))
    near = beside_b(att_near[2:4])
    z2c, o_bc = core(z2), core(o_b)

    o_zb, fresh = hold([o_zb, fresh], att_far, near, z2c, o_bc)
    far = beside_b(att_far[2:4])
    o_zbc = core(o_zb)
    fresh = sent_on(fresh, 1)
    total = out_own(att_near, att_far, qo, qo_c, z1, z1c, z2, z2c)
    mine, theirs = out_beside(place, inputs, total, near, far, o_b, o_bc, o_zb, o_zbc, fresh)

    onward = [(p, (p + 1) % (XS * ZS)) for p in range(XS * ZS)]
    across = [(y * XS * ZS + p, (y ^ 1) * XS * ZS + q) for p, q in onward for y in range(RING)]
    sums = [lax.ppermute(theirs, ("y",) + PIPE, across), lax.ppermute(mine, PIPE, onward)]
    passed = (sums[0].astype(F32) + sums[1].astype(F32)).astype(BF16)
    return (passed[None], fresh[None])


def solution(mesh):
    split = Mesh(mesh.devices.reshape(HALVES, RING, CORES, XS, ZS), SEQ + PIPE)
    placed = (
        P(PIPE, SEQ, None),
        P(PIPE, None),
        P(PIPE, None, SEQ),
        P(PIPE, None, SEQ),
        P(PIPE, SEQ, None),
        P(PIPE, SEQ, None),
        P(PIPE, None),
    )
    return jax.shard_map(
        per_device,
        mesh=split,
        in_specs=placed,
        out_specs=(P(PIPE, SEQ, None), P(PIPE, SEQ, None)),
        check_vma=False,
    )
```

```python
import functools

import jax
import jax.numpy as jnp
from jax import lax
from jax.experimental import pallas as pl
from jax.experimental.pallas import tpu as pltpu
from jax.sharding import Mesh
from jax.sharding import PartitionSpec as P

HALVES, RING, CORES, XS, ZS = 2, 4, 2, 4, 4
SEQ = ("zh", "y", "c")
PIPE = ("x", "zl")
rope_base = 500000.0
F32 = jnp.float32
BF16 = jnp.bfloat16
CHUNK = 1024


def prepare_kernel(acts, gain, first, out):
    wide = acts[...].astype(F32)
    scale = lax.rsqrt(jnp.mean(wide * wide, axis=-1, keepdims=True) + 1e-05)
    normed = (wide * scale * gain[...]).astype(BF16)
    lanes = lax.broadcasted_iota(jnp.int32, (acts.shape[0], 128), 1)
    for to in range(RING):
        out[to, :, :2048] = normed
        at = to // 2 * 128
        low = first[:, at : at + 128].astype(F32)
        high = first[:, 256 + at : 384 + at].astype(F32)
        if to % 2 == 0:
            high = pltpu.roll(high, 64, 1)
        else:
            low = pltpu.roll(low, 64, 1)
        out[to, :, 2048:] = jnp.where(lanes < 64, low, high).astype(BF16)


def pull(x, axis, by):
    n = lax.axis_size(axis)
    return lax.ppermute(x, axis, [((i + by) % n, i) for i in range(n)])


def rope_tables(positions, head_dim):
    half = head_dim // 2
    freq = rope_base ** (-2.0 * jnp.arange(half, dtype=F32) / head_dim)
    angle = positions.astype(F32)[:, None] * freq
    cosine, sine = jnp.cos(angle), jnp.sin(angle)
    return (
        jnp.concatenate([cosine] * 4, axis=-1),
        jnp.concatenate([-sine, sine, -sine, sine], axis=-1),
    )


def rope(u, cosine, sine):
    lanes = lax.broadcasted_iota(jnp.int32, u.shape, 1)
    swapped = jnp.where(lanes % 64 < 32, pltpu.roll(u, 96, 1), pltpu.roll(u, 32, 1))
    return u * cosine + swapped * sine


def keyval_kernel(place, x, mine, theirs, cos, sin, mix, *refs):
    kv_out, val_out, w = refs[-3:]
    h, c, section = place[1], place[2], place[3]
    w[0:64], w[64:128], w[128:192], w[192:256] = mine[0:64], theirs[0:64], mine[64:128], theirs[64:128]
    both = lax.dot_general(x[:, :2048], w[...], (((1,), (1,)), ((), ())), preferred_element_type=F32)
    rows = 128
    for slot in range(RING):
        part = both[slot * rows : (slot + 1) * rows]
        own, other = part[:, :128], part[:, 128:]
        keys = jnp.where(h == 0, own, other)
        values = jnp.where(h == 0, other, own)
        keys = jnp.where(c == 0, keys, pltpu.roll(keys, 64, 1))
        values = jnp.where(c == 0, values, pltpu.roll(values, 64, 1))
        rounded = values.astype(BF16)
        wide = rounded.astype(F32)
        before = jnp.where(section == 0, wide, x[slot * rows : (slot + 1) * rows, 2048:].astype(F32))
        mixed = mix[0:1, :] * wide + (1.0 - mix[0:1, :]) * before
        keys = rope(keys, cos[slot], sin[slot])
        lanes = lax.broadcasted_iota(jnp.int32, keys.shape, 1)
        low = jnp.where(lanes < 64, keys, pltpu.roll(mixed, 64, 1))
        high = jnp.where(lanes < 64, pltpu.roll(keys, 64, 1), mixed)
        kv_out[slot, :, 0:128] = low.astype(BF16)
        kv_out[slot, :, 128:256] = high.astype(BF16)
        val_out[slot] = rounded


def bundle_kernel(w_q, w_o, out):
    out[0] = w_q[...]
    for k in range(4):
        out[1, k * 128 : (k + 1) * 128, :] = w_o[:, k * 128 : (k + 1) * 128]


def query_kernel(x, wa, wb, cos, sin, out, w):
    w[:, :128], w[:, 128:] = wa[:2048], wb[:2048]
    both = jnp.dot(x[:, :2048], w[...], preferred_element_type=F32)
    for slot in range(RING):
        part = both[slot * 128 : (slot + 1) * 128]
        for pair in range(2):
            u = rope(part[:, pair * 128 : (pair + 1) * 128], cos[slot], sin[slot])
            out[slot, :, pair * 128 : (pair + 1) * 128] = (u * 0.125).astype(BF16)


def attend_kernel(place, q, kv, kv_c, before, before_c, *refs):
    out, keys, vals, scores, q4 = refs[-5:]
    step = pl.program_id(0)
    h, c = place[1], place[2]
    lanes = lax.broadcasted_iota(jnp.int32, (128, 128), 1)

    def place_block(src, k, half, core):
        both = src[k].astype(F32)
        turned = pltpu.roll(both, 64, 1)
        at = pl.ds(pl.multiple_of(half * 1024 + k * 256 + core * 128, 128), 128)
        keys[:, at] = jnp.where(lanes < 64, both, turned).T.astype(BF16)
        vals[at, :] = jnp.where(lanes < 64, turned, 1.0).astype(BF16)

    @pl.when(step == 0)
    def _():
        for k in range(RING):
            place_block(kv, k, h, c)
            place_block(kv_c, k, h, 1 - c)

    @pl.when((step == 0) & (h == 1))
    def _():
        for k in range(RING):
            place_block(before, k, 0, c)
            place_block(before_c, k, 0, 1 - c)

    for pair in range(2):
        block = q[0, :, pair * 128 : (pair + 1) * 128].astype(F32)
        q4[pair * 256 : pair * 256 + 128] = jnp.where(lanes < 64, block, 0.0).astype(BF16)
        q4[pair * 256 + 128 : pair * 256 + 256] = jnp.where(lanes < 64, 0.0, block).astype(BF16)
    last = h * (1024 // CHUNK) + step * 256 // CHUNK

    def dots(j):
        chunk = keys[:, pl.ds(pl.multiple_of(j * CHUNK, CHUNK), CHUNK)]
        return jnp.dot(q4[...], chunk, preferred_element_type=F32)

    def greatest(s):
        top = s[:, :128]
        for k in range(1, CHUNK // 128):
            top = jnp.maximum(top, s[:, k * 128 : (k + 1) * 128])
        return top

    s = dots(last)
    row = lax.rem(lax.broadcasted_iota(jnp.int32, s.shape, 0), 128) + c * 128 + lax.rem(step * 256, CHUNK)
    col = lax.broadcasted_iota(jnp.int32, s.shape, 1)
    s = jnp.where(col <= row, s, -1e30)
    scores[last] = s

    def first_pass(j, top):
        s = dots(j)
        scores[j] = s
        return jnp.maximum(top, greatest(s))

    top = lax.fori_loop(0, last, first_pass, greatest(s))
    top = jnp.max(top, axis=1, keepdims=True)

    def second_pass(j, acc):
        p = jnp.exp(scores[j] - top).astype(BF16)
        chunk = vals[pl.ds(pl.multiple_of(j * CHUNK, CHUNK), CHUNK), :]
        return acc + jnp.dot(p, chunk, preferred_element_type=F32)

    acc = lax.fori_loop(0, last + 1, second_pass, jnp.zeros((512, 128), F32))
    result = acc / pltpu.roll(acc, 64, 1)
    for pair in range(2):
        left = result[pair * 256 : pair * 256 + 128]
        right = pltpu.roll(result[pair * 256 + 128 : pair * 256 + 256], 64, 1)
        out[0, :, pair * 128 : (pair + 1) * 128] = jnp.where(lanes < 64, left, right).astype(BF16)


def gather_heads_kernel(place, parts, out):
    lanes = lax.broadcasted_iota(jnp.int32, (128, 128), 1)
    keep = jnp.where(place[3] == 0, 1.0, 0.0)
    for k in range(0, RING, 2):
        left, right = parts[k].astype(F32) * keep, parts[k + 1].astype(F32) * keep
        at = k // 2 * 128
        out[:, at : at + 128] = jnp.where(lanes < 64, left, pltpu.roll(right, 64, 1)).astype(BF16)
        out[:, 256 + at : 384 + at] = jnp.where(lanes < 64, pltpu.roll(left, 64, 1), right).astype(BF16)


def times_rows(att, wa, wb, w):
    for half, pieces in enumerate((wa, wb)):
        at = 0
        for piece, begin in pieces:
            for row in range(begin, piece.shape[0], 128):
                w[half * 128 : half * 128 + 128, at : at + 128] = piece[row : row + 128, :]
                at += 128
    return jnp.dot(att.reshape(256, 256), w[...], preferred_element_type=F32)


def out_own_kernel(near, far, qo, qo_c, z1, z1c, z2, z2c, total, w):
    total[...] = times_rows(near[0:2], [(qo, 2048)], [(qo_c, 2048)], w)
    total[...] += times_rows(far[0:2], [(z1, 2048), (z2, 0)], [(z1c, 2048), (z2c, 0)], w)


def out_beside_kernel(place, acts, base, near, far, o_b, o_bc, o_zb, o_zbc, fresh, mine, theirs, w):
    odd = lax.rem(place[0], 2)
    total = base[...] + times_rows(near[...], [(o_b, 0)], [(o_bc, 0)], w)
    total += times_rows(far[...], [(o_zb, 0)], [(o_zbc, 0)], w)
    low, high = total[:128], total[128:]
    mine[...] = (acts[...].astype(F32) + jnp.where(odd == 0, low, high)).astype(BF16)
    theirs[...] = jnp.where(odd == 0, high, low).astype(BF16)


def params(mib):
    return pltpu.CompilerParams(vmem_limit_bytes=mib * 2**20)


VM = pl.BlockSpec(memory_space=pltpu.VMEM)
SM = pl.BlockSpec(memory_space=pltpu.SMEM)


def prepare(acts, gain, first):
    return pl.pallas_call(
        prepare_kernel,
        out_shape=jax.ShapeDtypeStruct((RING, acts.shape[0], 2048 + 128), BF16),
        grid=(4,),
        in_specs=[
            pl.BlockSpec((32, 2048), lambda i: (i, 0)),
            pl.BlockSpec((1, 2048), lambda i: (0, 0)),
            pl.BlockSpec((32, 512), lambda i: (i, 0)),
        ],
        out_specs=pl.BlockSpec((RING, 32, 2048 + 128), lambda i: (0, i, 0)),
        compiler_params=params(16),
        cost_estimate=pl.CostEstimate(flops=2 * 512 * 2048 * 256, bytes_accessed=4 << 20, transcendentals=0),
    )(acts, gain, first)


def keyval(operands, *others):
    return pl.pallas_call(
        keyval_kernel,
        out_shape=(jax.ShapeDtypeStruct((4, 128, 256), BF16), jax.ShapeDtypeStruct((4, 128, 128), BF16)),
        in_specs=[SM] + [VM] * 6 + [pl.BlockSpec(memory_space=pl.ANY)] * len(others),
        out_specs=(VM, VM),
        scratch_shapes=[pltpu.VMEM((256, 2048), BF16)],
        compiler_params=params(24),
        cost_estimate=pl.CostEstimate(flops=2 * 512 * 2048 * 256, bytes_accessed=4 << 20, transcendentals=0),
    )(*operands, *others)


def query(x, wa, wb, cos, sin):
    return pl.pallas_call(
        query_kernel,
        out_shape=jax.ShapeDtypeStruct((4, 128, 256), BF16),
        in_specs=[VM] * 5,
        out_specs=VM,
        scratch_shapes=[pltpu.VMEM((2048, 256), BF16)],
        compiler_params=params(24),
        cost_estimate=pl.CostEstimate(flops=2 * 512 * 2048 * 256, bytes_accessed=4 << 20, transcendentals=0),
    )(x, wa, wb, cos, sin)


def attend(place, q, kvs, *others):
    def at(step, place):
        return (step, 0, 0)

    def to(step, place):
        return (lax.rem(step + place[0] // 2 * 2, RING), 0, 0)

    return pl.pallas_call(
        attend_kernel,
        out_shape=jax.ShapeDtypeStruct((4, 128, 256), BF16),
        grid_spec=pltpu.PrefetchScalarGridSpec(
            num_scalar_prefetch=1,
            grid=(RING,),
            in_specs=[
                pl.BlockSpec((1, 128, 256), at),
            ]
            + [pl.BlockSpec((RING, 128, 128), lambda step, place: (0, 0, place[4]))] * 4
            + [pl.BlockSpec(memory_space=pl.ANY)] * len(others),
            out_specs=pl.BlockSpec((1, 128, 256), to),
            scratch_shapes=[
                pltpu.VMEM((128, 2048), BF16),
                pltpu.VMEM((2048, 128), BF16),
                pltpu.VMEM((2048 // CHUNK, 512, CHUNK), F32),
                pltpu.VMEM((512, 128), BF16),
            ],
        ),
        compiler_params=params(24),
        cost_estimate=pl.CostEstimate(flops=2 * 2 * 512 * 256 * 6656, bytes_accessed=32 << 20, transcendentals=512 * 6656),
    )(place, q, *kvs, *others)


def bundle(w_q, w_o):
    return pl.pallas_call(
        bundle_kernel,
        out_shape=jax.ShapeDtypeStruct((2, 2048, 128), BF16),
        grid=(4,),
        in_specs=[pl.BlockSpec((512, 128), lambda i: (i, 0)), pl.BlockSpec((128, 512), lambda i: (0, i))],
        out_specs=pl.BlockSpec((2, 512, 128), lambda i: (0, i, 0)),
        compiler_params=params(16),
        cost_estimate=pl.CostEstimate(flops=0, bytes_accessed=2 << 20, transcendentals=0),
    )(w_q, w_o)


def out_own(*operands):
    return pl.pallas_call(
        out_own_kernel,
        out_shape=jax.ShapeDtypeStruct((256, 2048), F32),
        in_specs=[VM] * 8,
        out_specs=VM,
        scratch_shapes=[pltpu.VMEM((256, 2048), BF16)],
        compiler_params=params(32),
        cost_estimate=pl.CostEstimate(flops=2 * 256 * 512 * 2048, bytes_accessed=4 << 20, transcendentals=0),
    )(*operands)


def out_beside(*operands):
    return pl.pallas_call(
        out_beside_kernel,
        out_shape=(jax.ShapeDtypeStruct((128, 2048), BF16),) * 2,
        in_specs=[SM] + [VM] * 8 + [pl.BlockSpec(memory_space=pl.ANY)],
        out_specs=(VM, VM),
        scratch_shapes=[pltpu.VMEM((256, 2048), BF16)],
        compiler_params=params(32),
        cost_estimate=pl.CostEstimate(flops=2 * 256 * 512 * 2048, bytes_accessed=4 << 20, transcendentals=0),
    )(*operands)


def hold(arrays, *others):
    n = len(arrays)
    return pl.pallas_call(
        lambda *refs: None,
        out_shape=[jax.ShapeDtypeStruct(x.shape, x.dtype) for x in arrays],
        in_specs=[pl.BlockSpec(memory_space=pl.ANY)] * (n + len(others)),
        out_specs=[pl.BlockSpec(memory_space=pl.ANY)] * n,
        input_output_aliases={k: k for k in range(n)},
    )(*arrays, *others)


def gather_heads(place, parts):
    return pl.pallas_call(
        gather_heads_kernel,
        out_shape=jax.ShapeDtypeStruct((128, 512), BF16),
        in_specs=[SM, VM],
        out_specs=VM,
        cost_estimate=pl.CostEstimate(flops=0, bytes_accessed=1 << 18, transcendentals=0),
    )(place, parts)


def beside_b(x):
    return lax.ppermute(x, "y", [(y, RING - 1 - y) for y in range(RING)])


def swap(x):
    return lax.all_to_all(x, "y", 0, 0)


def per_device(acts, norm_gain, query_weight, kv_weight, out_weight, first_values, mix_weight):
    inputs = acts[0]
    tok = inputs.shape[0]
    h, y, c = lax.axis_index("zh"), lax.axis_index("y"), lax.axis_index("c")
    section = lax.axis_index("x") * ZS + lax.axis_index("zl")
    place = jnp.stack([y, h, c, section, h]).astype(jnp.int32)
    place_far = jnp.stack([y, h, c, section, 1 - h]).astype(jnp.int32)
    core = functools.partial(pull, axis="c", by=1)
    half = functools.partial(pull, axis="zh", by=1)

    positions = h * 8 * tok + (2 * jnp.arange(RING, dtype=jnp.int32)[:, None] + c) * tok + jnp.arange(tok, dtype=jnp.int32)
    cos, sin = (t.reshape(RING, tok, 128) for t in rope_tables(positions.reshape(-1), 64))
    mix_two = lax.dynamic_index_in_dim(mix_weight[0].reshape(2, RING), y, 1, keepdims=False)
    mix = jnp.broadcast_to(jnp.repeat(mix_two, 64)[None, :], (8, 128))

    x = swap(prepare(inputs, norm_gain, first_values[0]))

    w_kv = kv_weight[0].T
    home = [(s, s // 8 * 8 + s % 4 * 2 + s % 8 // 4) for s in range(16)]
    kv_b = lax.ppermute(w_kv, SEQ, [(s, (d + 8) % 16) for s, d in home])
    kv_a = lax.ppermute(w_kv, SEQ, home)
    mine = jnp.concatenate([kv_a, kv_b], axis=0)
    theirs = core(mine)

    qo = bundle(query_weight[0], out_weight[0])
    qo = qo.reshape(4096, 128)
    z1, qo_c = half(qo[:3072]), core(qo)
    x = x.reshape(RING * tok, 2048 + 128)
    kv, values = keyval((place, x, mine, theirs, cos, sin, mix))

    kv_c = core(kv)
    kv_before = lax.ppermute(kv, "zh", [(0, 1)])
    q_near = query(x, qo, qo_c, cos, sin)
    fresh = gather_heads(place, swap(values))
    kv_before, o_2 = hold([kv_before, qo[3072:]], q_near, fresh)
    kv_before_c = core(kv_before)
    kvs = (kv, kv_c, kv_before, kv_before_c)

    kv_before, o_2 = hold([kv_before, qo[3072:]], q_near, fresh)
    kv_before_c = core(kv_before)
    kvs = (kv, kv_c, kv_before, kv_before_c)

    def sent_on(x, stride):
        return [lax.ppermute(x, PIPE, [(p, p + k * stride) for p in range(stride)]) for k in range(1, 4)]

    def sent_on(x, *rounds):
        return sum([lax.ppermute(x, PIPE, pairs) for pairs in rounds], x)

    z1, o_own, fresh = hold([z1, qo[2048:], fresh], kv_before_c)
    fresh = sent_on(fresh, [(0, 2)])
    z2 = half(o_2)
    o_b = beside_b(o_own)
    att_near = attend(place, q_near, kvs)
    z1c = core(z1)
    q_far = query(x, z1, z1c, cos, sin)

    q_far, z2, o_b, fresh = hold([q_far, z2, o_b, fresh], att_near)
    fresh = sent_on(fresh, [(0, 1), (2, 3)])
    att_far = attend(place_far, q_far, kvs)
    o_zb = beside_b(jnp.concatenate([z1[2048:], z2], axis=0))
    near = beside_b(att_near[2:4])
    z2c, o_bc = core(z2), core(o_b)

    o_zb, fresh = hold([o_zb, fresh], att_far, near, z2c, o_bc)
    far = beside_b(att_far[2:4])
    o_zbc = core(o_zb)
    fresh = sent_on(fresh, *[[(p, p + k * ZS) for p in range(ZS)] for k in range(1, XS)])
    total = out_own(att_near, att_far, qo, qo_c, z1, z1c, z2, z2c)
    mine, theirs = out_beside(place, inputs, total, near, far, o_b, o_bc, o_zb, o_zbc, fresh)

    onward = [(p, (p + 1) % (XS * ZS)) for p in range(XS * ZS)]
    across = [(y * XS * ZS + p, (y ^ 1) * XS * ZS + q) for p, q in onward for y in range(RING)]
    sums = [lax.ppermute(theirs, ("y",) + PIPE, across), lax.ppermute(mine, PIPE, onward)]
    passed = (sums[0].astype(F32) + sums[1].astype(F32)).astype(BF16)
    return (passed[None], fresh[None])


def solution(mesh):
    split = Mesh(mesh.devices.reshape(HALVES, RING, CORES, XS, ZS), SEQ + PIPE)
    placed = (
        P(PIPE, SEQ, None),
        P(PIPE, None),
        P(PIPE, None, SEQ),
        P(PIPE, None, SEQ),
        P(PIPE, SEQ, None),
        P(PIPE, SEQ, None),
        P(PIPE, None),
    )
    return jax.shard_map(
        per_device,
        mesh=split,
        in_specs=placed,
        out_specs=(P(PIPE, SEQ, None), P(PIPE, SEQ, None)),
        check_vma=False,
    )
```
